256 devices in a mesh: ctx: 32 (over z, x), head: 8 (over y, core).
Axes of the slice: x: 4, y: 4, z: 8, core: 2. Of those that a mesh axis runs over, the one named last changes fastest.
Arguments:
- queries: bfloat16 [4096, 4096], P('ctx', 'head'), may hold values from -0.625 to 0.625
- key_vectors: bfloat16 [4096, 4096], P('ctx', 'head'), may hold values from -1.75 to 1.75
- value_vectors: bfloat16 [4096, 4096], P('ctx', 'head'), may hold values from -6 to 6
- out_grad: bfloat16 [4096, 6144], P('ctx', 'head'), may hold values from -1.25 to 1.25
- out_weight: bfloat16 [6144, 4096], P(None, 'head'), may hold values from -0.09375 to 0.09375
- decay_rate: float32 [32], P('head'), may hold values from 2.4414063e-05 to 0.08, as said below
Outputs:
- query_grad: bfloat16 [4096, 4096], P('ctx', 'head')
- key_grad: bfloat16 [4096, 4096], P('ctx', 'head')
- value_grad: bfloat16 [4096, 4096], P('ctx', 'head')
- weight_grad: float32 [6144, 4096], P('ctx', 'head')
The draws below stay inside these ranges and needn't reach their ends.
Inputs may be any that keep to these rules, and one draw needn't show every extreme that they name: decay_rate[h] is the rate r of head h: its state is multiplied by exp(-r) at each position.
All inputs are finite; a program needn't handle non-finite values.
Results may differ from the reference program's by a relative error of at most 0.0064.
Values may be sent and summed in bfloat16 or wider, within the bound.
A program may use at most 128 MiB of HBM per device.

```python
import math
import jax
import jax.numpy as jnp
from jax import lax

D = 6144
HEADS = 32
E = 128
TOK_DEV = 128
TOKENS = 4096


def draw_decay_rate(key, part):
    key = jax.random.fold_in(key, 11)
    key_slow, key_middle, key_fast, key_order = jax.random.split(key, 4)
    slow_rates = jnp.exp(jax.random.uniform(key_slow, (HEADS,), jnp.float32, math.log(0.1), math.log(2.0))) / TOKENS
    middle_rates = jnp.exp(jax.random.uniform(key_middle, (HEADS,), jnp.float32, math.log(1.02), math.log(1.25))) / min(TOK_DEV, 512)
    fast_rates = jnp.exp(jax.random.uniform(key_fast, (HEADS,), jnp.float32, math.log(0.02), math.log(0.08)))
    ranking = jax.random.permutation(key_order, HEADS)
    slow_count = HEADS // 2
    middle_count = HEADS // 4
    rates = jnp.where(ranking < slow_count + middle_count, middle_rates, fast_rates)
    rates = jnp.where(ranking < slow_count, slow_rates, rates)
    return rates.astype(jnp.float32)


def strengthened(result, rng, source, target, parts, factor):
    owner, partner = [(jnp.arange(result.shape[dim]) // (result.shape[dim] // parts)).reshape([-1 if axis == dim else 1 for axis in range(result.ndim)]) for dim in (source, target)]
    chosen = jax.random.permutation(rng, parts)[partner]
    strong = (owner == chosen) | (owner == (partner + parts // 2) % parts)
    return jnp.where(strong, factor * result, result)


def level_of(rng, extent, shards, low, largest):
    level, own = 1.0, jax.random.fold_in(rng, 6)
    for axis_at, shards_of in shards:
        draws = jnp.exp(jax.random.uniform(jax.random.fold_in(own, axis_at), (shards_of,), jnp.float32, low / len(shards), largest / len(shards)))
        level = level * jnp.repeat(draws, extent[axis_at] // shards_of).reshape([-1 if axis == axis_at else 1 for axis in range(len(extent))])
    return level


def gaussian(key, extent, deviation, reach, shards=(), kind=jnp.bfloat16):
    factor_of = level_of(key, extent, shards, -0.22, 0.18) if shards else 1.0
    entries = jax.random.normal(key, extent, jnp.float32) * deviation * factor_of
    return jnp.minimum(jnp.maximum(entries, -reach), reach).astype(kind)


def noise_with(stream_key, extent, scale, bound, cuts, heavy, held_as=jnp.bfloat16):
    entries = scale * jax.random.normal(stream_key, extent, jnp.float32)
    if cuts:
        entries = entries * level_of(stream_key, extent, cuts, -0.22, 0.18)
    return jnp.clip(strengthened(entries, jax.random.fold_in(stream_key, 3), *heavy), -bound, bound).astype(held_as)


def setup_inputs(seed: int = 0) -> dict:
    arg_keys = jax.random.split(jax.random.key(seed), 7)
    return {
        "queries": gaussian(arg_keys[0], (TOKENS, HEADS * E), 0.1, 0.625, ((0, 32), (1, 8))),
        "key_vectors": gaussian(arg_keys[1], (TOKENS, HEADS * E), 0.3, 1.75, ((0, 32), (1, 8))),
        "value_vectors": gaussian(arg_keys[2], (TOKENS, HEADS * E), 1.0, 6.0, ((0, 32), (1, 8))),
        "out_grad": noise_with(arg_keys[3], (TOKENS, D), 0.1, 1.25, ((0, 32), (1, 8)), (0, 1, 32, 2.75)),
        "out_weight": gaussian(arg_keys[4], (D, HEADS * E), (HEADS * E) ** -0.5, 0.09375, ((1, 8),)),
        "decay_rate": draw_decay_rate(jax.random.fold_in(arg_keys[6], 71), 0),
    }


def product(form, left, right):
    return jnp.einsum(form, left.astype(jnp.float32), right.astype(jnp.float32),
                      precision=lax.Precision.HIGHEST)


def head_pass(head_items):
    query_head, key_head, value_head, grad_head, rate_value = head_items
    block_rows = min(TOK_DEV, 512)
    block_count = TOKENS // block_rows
    q_blocks = query_head.reshape(block_count, block_rows, E)
    k_blocks = key_head.reshape(block_count, block_rows, E)
    v_blocks = value_head.reshape(block_count, block_rows, E)
    g_blocks = grad_head.reshape(block_count, block_rows, E)
    offsets = jnp.arange(block_rows, dtype=jnp.float32)
    distance = offsets[:, None] - offsets[None, :]
    weights = jnp.where(distance >= 0, jnp.exp(-rate_value * jnp.maximum(distance, 0.0)), 0.0)
    in_decay = jnp.exp(-rate_value * (offsets + 1.0))[None, :, None]
    out_decay = jnp.exp(-rate_value * (block_rows - 1.0 - offsets))[None, :, None]
    back_decay = jnp.exp(-rate_value * (block_rows - offsets))[None, :, None]
    tok_decay = jnp.exp(-rate_value * offsets)[None, :, None]
    step_decay = jnp.exp(-rate_value * block_rows)
    scores = (product('nte,nse->nts', q_blocks, k_blocks) * weights[None]).astype(jnp.bfloat16)
    grad_scores = (product('ntf,nsf->nts', g_blocks, v_blocks) * weights[None]).astype(jnp.bfloat16)
    keys_decayed = (k_blocks.astype(jnp.float32) * out_decay).astype(jnp.bfloat16)
    queries_decayed = (q_blocks.astype(jnp.float32) * tok_decay).astype(jnp.bfloat16)
    kv_terms = product('nse,nsf->nef', keys_decayed, v_blocks)
    qg_terms = product('nte,ntf->nef', queries_decayed, g_blocks)

    def advance(running, term_rows):
        return step_decay * running + term_rows, running

    zero_state = jnp.zeros((E, E), jnp.float32)
    _, starts = lax.scan(advance, zero_state, kv_terms)
    _, ends = lax.scan(advance, zero_state, qg_terms, reverse=True)
    starts = starts.astype(jnp.bfloat16)
    ends = ends.astype(jnp.bfloat16)
    attention_out = in_decay * product('nte,nef->ntf', q_blocks, starts)
    attention_out = attention_out + product('nts,nsf->ntf', scores, v_blocks)
    query_grad = in_decay * product('ntf,nef->nte', g_blocks, starts)
    query_grad = query_grad + product('nts,nse->nte', grad_scores, k_blocks)
    key_grad = back_decay * product('nsf,nef->nse', v_blocks, ends)
    key_grad = key_grad + product('nts,nte->nse', grad_scores, q_blocks)
    value_grad = back_decay * product('nse,nef->nsf', k_blocks, ends)
    value_grad = value_grad + product('nts,ntf->nsf', scores, g_blocks)
    return (attention_out.reshape(TOKENS, E), query_grad.reshape(TOKENS, E),
            key_grad.reshape(TOKENS, E), value_grad.reshape(TOKENS, E))


def reference(queries, key_vectors, value_vectors, out_grad, out_weight, decay_rate):
    head_grad = jnp.dot(out_grad, out_weight, preferred_element_type=jnp.float32).astype(jnp.bfloat16)

    def by_head(tensor):
        return tensor.reshape(TOKENS, HEADS, E).transpose(1, 0, 2)

    def join_heads(tensor):
        return tensor.transpose(1, 0, 2).reshape(TOKENS, HEADS * E).astype(jnp.bfloat16)

    results = lax.map(head_pass, (by_head(queries), by_head(key_vectors), by_head(value_vectors),
                                  by_head(head_grad), decay_rate))
    attention_out = join_heads(results[0])
    weight_grad = jnp.dot(out_grad.T, attention_out, preferred_element_type=jnp.float32)
    return join_heads(results[1]), join_heads(results[2]), join_heads(results[3]), weight_grad
```

```python
import functools

import jax
import jax.numpy as jnp
from jax import lax
from jax.experimental import pallas as pl
from jax.experimental.pallas import tpu as pltpu
from jax.sharding import PartitionSpec as P

E = 128
X = 4
MESH = pl.DeviceIdType.MESH
F32 = jnp.float32
BF16 = jnp.bfloat16


def dot(a, b, ca=1, cb=0):
    return lax.dot_general(a, b, (((ca,), (cb,)), ((), ())), preferred_element_type=F32)


def kernel(Z, Y, r_ref, q_hbm, k_hbm, v_hbm, og_hbm, w_hbm, qg_ref, kg_ref, vg_ref, wg_ref,
           q, k, v, w, fg, gz, gzt, hg, hacc, sc, gs, ts, tx, rs, rz, ss, st, acc, ab, dws, dwr,
           local_sem, g_send, g_recv, p_send, p_recv, t_send, t_recv, r_send, r_recv,
           s_send, s_recv, a_send, a_recv, d_send, d_recv):
    B = q.shape[0]
    D8 = fg.shape[2]
    CH = D8 // X
    H = 2 * Y
    PIECE = B // H
    ctx = lax.axis_index("ctx")
    h = lax.axis_index("head")
    z, x = ctx // X, lax.rem(ctx, X)
    y, c = h // 2, lax.rem(h, 2)

    def at_z(zz):
        return (lax.rem(zz + Z, Z) * X + x, h)

    def at_x(xx):
        return (z * X + xx, h)

    def yhead(dy, cc):
        return lax.rem(y + dy + Y, Y) * 2 + cc

    def at_h(hh):
        return (ctx, hh)

    sib = 1 - c

    def remote(src, dst, send, recv, to):
        return pltpu.make_async_remote_copy(
            src_ref=src, dst_ref=dst, send_sem=send, recv_sem=recv, device_id=to, device_id_type=MESH)

    loads = [pltpu.make_async_copy(a, b, local_sem.at[i]) for i, (a, b) in enumerate(
        ((k_hbm, k), (v_hbm, v), (q_hbm, q), (og_hbm, fg.at[h]), (w_hbm, w)))]
    for load in loads:
        load.start()
    barrier = pltpu.get_barrier_semaphore()
    peers = ([at_z(z + d) for d in range(1, Z)] + [at_x(lax.rem(x + o, X)) for o in range(1, X)]
             + [at_h(yhead(1, c)), at_h(yhead(-1, c)), at_h(yhead(0, sib))])
    for peer in peers:
        pl.semaphore_signal(barrier, inc=1, device_id=peer, device_id_type=MESH)

    rows = lax.broadcasted_iota(jnp.int32, (B, E), 0).astype(F32)
    dist = (lax.broadcasted_iota(jnp.int32, (B, B), 0)
            - lax.broadcasted_iota(jnp.int32, (B, B), 1)).astype(F32)

    def head(ref, j):
        return ref[:, j * E:(j + 1) * E]

    def weights(j):
        return jnp.where(dist >= 0, jnp.exp(-r_ref[j] * jnp.maximum(dist, 0.0)), 0.0)

    def power(rate, count):
        return jnp.exp(jnp.full((1, E), -rate * count, F32))

    def scan_send(g):
        for o in range(1, X):
            peer = lax.rem(x + o, X)
            remote(ts.at[g, peer], tx.at[g, x], t_send.at[g, o - 1], t_recv.at[g, o - 1], at_x(peer)).start()
        tx[g, x] = ts[g, x]

    r_own = r_ref[x]

    def scan_rows(g):
        for o in range(1, X):
            src = lax.rem(x - o + X, X)
            remote(ts.at[g, src], tx.at[g, src], t_send.at[g, o - 1], t_recv.at[g, o - 1], at_x(src)).wait_recv()
        total = jnp.zeros((E, E), F32)
        for xx in range(X):
            away = xx if g else X - 1 - xx
            total = total + power(r_own, float(B * away)) * tx[g, xx].astype(F32)
        rs[g] = total.astype(BF16)
        for d in range(1, Z):
            there = z - d if g else z + d

            @pl.when((there >= 0) & (there < Z))
            def _():
                remote(rs.at[g], rz.at[g, z], r_send.at[g, d - 1], r_recv.at[g, d - 1], at_z(there)).start()

    def scan_finish(g):
        acc[...] = jnp.zeros((E, E), F32)
        for d in range(1, Z):
            src = z + d if g else z - d

            @pl.when((src >= 0) & (src < Z))
            def _():
                remote(rs.at[g], rz.at[g, src], r_send.at[g, d - 1], r_recv.at[g, d - 1], at_z(src)).wait_recv()
                acc[...] += power(r_own, float(X * B * (d - 1))) * rz[g, src].astype(F32)

        state = acc[...]
        step = power(r_own, float(B))
        for xx in (reversed(range(X)) if g else range(X)):
            ss[g, xx] = state.astype(BF16)
            state = step * state + tx[g, xx].astype(F32)
        for o in range(1, X):
            peer = lax.rem(x + o, X)
            remote(ss.at[g, peer], st.at[g, x], s_send.at[g, o - 1], s_recv.at[g, o - 1], at_x(peer)).start()
        st[g, x] = ss[g, x]

    def scan_wait(g):
        for o in range(1, X):
            src = lax.rem(x - o + X, X)
            remote(ss.at[g, src], st.at[g, src], s_send.at[g, o - 1], s_recv.at[g, o - 1], at_x(src)).wait_recv()

    def piece(n, hh, half=None):
        if n == 0:
            if half is None:
                return fg.at[hh]
            return fg.at[hh, half * (B // 2):(half + 1) * (B // 2), :]
        mine = pl.ds(pl.multiple_of(hh * PIECE, PIECE), PIECE)
        if half is None:
            return gz.at[:, mine, :]
        return gz.at[half * (Z // 2):(half + 1) * (Z // 2), mine, :]

    def hop(n, hh, half, i, to):
        ref = piece(n, hh, half)
        return remote(ref, ref, g_send.at[n, i], g_recv.at[n, i], at_h(to))

    up, down = yhead(1, c), yhead(-1, c)
    far = yhead(2, c)
    across = yhead(0, sib)

    def gather_start(n):
        hop(n, h, 0, 0, up).start()
        hop(n, h, 1, 1, down).start()
        hop(n, h, None, 6, across).start()
        hop(n, h, 1, 2, up).start()
        hop(n, h, 0, 3, down).start()

    def gather_forward(n):
        hop(n, down, 0, 0, up).wait_recv()
        hop(n, down, 0, 4, up).start()
        hop(n, up, 1, 1, down).wait_recv()
        hop(n, up, 1, 5, down).start()

    def gather_near(n):
        hop(n, down, 1, 2, up).wait_recv()
        hop(n, down, None, 7, across).start()
        hop(n, up, 0, 3, down).wait_recv()
        hop(n, up, None, 8, across).start()

    def gather_far(n):
        hop(n, far, 0, 4, up).wait_recv()
        hop(n, far, 1, 5, down).wait_recv()
        hop(n, far, None, 9, across).start()

    def gather_across(n, i):
        hh = yhead((0, -1, 1, 2)[i], sib)
        hop(n, hh, None, 6 + i, across).wait_recv()
        return hh

    my_piece = pl.ds(pl.multiple_of(h * PIECE, PIECE), PIECE)

    def pass_piece(zz):
        @pl.when(zz != z)
        def _():
            remote(fg.at[zz, my_piece, :], gz.at[z, my_piece, :], p_send.at[zz], p_recv.at[z], at_z(zz)).start()

        @pl.when(zz == z)
        def _():
            gz[z, my_piece, :] = fg[zz, my_piece, :]

    hops = ((Z // 2, Z - 1 - Z // 2), (Z - 1 - Z // 2, Z // 2))

    def ring(s):
        for p in range(2):
            for way in range(2):
                sign = -1 if way else 1
                if 0 < s <= hops[p][way]:
                    came = lax.rem(z - sign * s + Z, Z)
                    remote(ab.at[p, came], ab.at[p, came], a_send.at[p, way, s - 1],
                           a_recv.at[p, way, s - 1], at_z(z + sign)).wait_recv()
                if s < hops[p][way]:
                    block = lax.rem(z - sign * s + Z, Z)
                    remote(ab.at[p, block], ab.at[p, block], a_send.at[p, way, s],
                           a_recv.at[p, way, s], at_z(z + sign)).start()

    for load in loads[:3]:
        load.wait()
    for j in range(X):
        decayed = (head(k, j).astype(F32) * jnp.exp(-r_ref[j] * (B - 1.0 - rows))).astype(BF16)
        ts[0, j] = dot(decayed, head(v, j), 0, 0).astype(BF16)
    loads[3].wait()
    pl.semaphore_wait(barrier, len(peers))

    scan_send(0)
    gather_start(0)
    pass_piece(h)
    for j in range(X):
        sc[j] = (dot(head(q, j), head(k, j), 1, 1) * weights(j)).astype(BF16)
    scan_rows(0)
    pass_piece(gather_across(0, 0))
    gather_forward(0)
    gather_near(0)
    pass_piece(down)
    pass_piece(up)
    pass_piece(gather_across(0, 1))
    pass_piece(gather_across(0, 2))
    scan_finish(0)
    gather_far(0)
    pass_piece(far)
    pass_piece(gather_across(0, 3))

    loads[4].wait()
    hacc[...] = jnp.zeros_like(hacc)

    def part(i, carry):
        hacc[...] += dot(fg[i], w[pl.ds(pl.multiple_of(i * D8, D8), D8), :])
        return carry

    lax.fori_loop(0, H, part, 0)
    hg[...] = hacc[...].astype(BF16)

    scan_wait(0)
    for j in range(X):
        inter = jnp.exp(-r_ref[j] * (rows + 1.0)) * dot(head(q, j), st[0, j])
        ab[j // 2, z, :, (j % 2) * E:(j % 2 + 1) * E] = (inter + dot(sc[j], head(v, j))).astype(BF16)
    ring(0)
    for j in range(X):
        decayed = (head(q, j).astype(F32) * jnp.exp(-r_ref[j] * rows)).astype(BF16)
        ts[1, j] = dot(decayed, head(hg, j), 0, 0).astype(BF16)
    scan_send(1)
    for zz in range(Z):
        @pl.when(zz != z)
        def _():
            remote(gz.at[zz, my_piece, :], gz.at[zz, my_piece, :], p_send.at[zz], p_recv.at[zz], at_z(zz)).wait_recv()
    gather_start(1)
    ring(1)
    scan_rows(1)
    gather_forward(1)
    ring(2)
    for j in range(X):
        gs[j] = (dot(head(hg, j), head(v, j), 1, 1) * weights(j)).astype(BF16)
        inter = jnp.exp(-r_ref[j] * (rows + 1.0)) * dot(head(hg, j), st[0, j], 1, 1)
        qg_ref[:, j * E:(j + 1) * E] = (inter + dot(gs[j], head(k, j))).astype(BF16)
    gather_near(1)
    ring(3)
    gather_far(1)
    for i in range(4):
        gather_across(1, i)
    for zz in range(Z):
        gzt[:, zz * B:(zz + 1) * B] = gz[zz].T
    scan_finish(1)
    for s in range(4, max(max(n) for n in hops) + 1):
        ring(s)

    def rows_of(xx):
        return gzt[pl.ds(pl.multiple_of(xx * CH, CH), CH), :]

    for p in range(2):
        right = ab[p].reshape(Z * B, 2 * E)
        for o in (2, 1, 3):
            peer = lax.rem(x + o, X)
            dws[p, o - 1] = dot(rows_of(peer), right).astype(BF16)
            remote(dws.at[p, o - 1], dwr.at[p, o - 1], d_send.at[p, o - 1], d_recv.at[p, o - 1], at_x(peer)).start()
    for p in range(2):
        wg_ref[:, p * 2 * E:(p + 1) * 2 * E] = dot(rows_of(x), ab[p].reshape(Z * B, 2 * E))
    scan_wait(1)
    for j in range(X):
        back = jnp.exp(-r_ref[j] * (B - rows))
        kg_ref[:, j * E:(j + 1) * E] = (
            back * dot(head(v, j), st[1, j], 1, 1) + dot(gs[j], head(q, j), 0, 0)).astype(BF16)
        vg_ref[:, j * E:(j + 1) * E] = (
            back * dot(head(k, j), st[1, j]) + dot(sc[j], head(hg, j), 0, 0)).astype(BF16)
    for p in range(2):
        for o in (1, 3, 2):
            src = lax.rem(x - o + X, X)
            remote(dws.at[p, o - 1], dwr.at[p, o - 1], d_send.at[p, o - 1], d_recv.at[p, o - 1], at_x(src)).wait_recv()
            wg_ref[:, p * 2 * E:(p + 1) * 2 * E] += dwr[p, o - 1].astype(F32)

    for g in range(2):
        for o in range(1, X):
            remote(ts.at[g, 0], tx.at[g, 0], t_send.at[g, o - 1], t_recv.at[g, o - 1], at_x(x)).wait_send()
            remote(ss.at[g, 0], st.at[g, 0], s_send.at[g, o - 1], s_recv.at[g, o - 1], at_x(x)).wait_send()
        for d in range(1, Z):
            there = z - d if g else z + d

            @pl.when((there >= 0) & (there < Z))
            def _():
                remote(rs.at[g], rz.at[g, z], r_send.at[g, d - 1], r_recv.at[g, d - 1], at_z(there)).wait_send()
    for n in range(2):
        for i, half in enumerate((0, 1, 1, 0, 0, 1, None, None, None, None)):
            hop(n, h, half, i, up).wait_send()
    for zz in range(Z):
        @pl.when(zz != z)
        def _():
            remote(fg.at[zz, my_piece, :], gz.at[z, my_piece, :], p_send.at[zz], p_recv.at[z], at_z(zz)).wait_send()
    for p in range(2):
        for way in range(2):
            for s in range(hops[p][way]):
                remote(ab.at[p, z], ab.at[p, z], a_send.at[p, way, s], a_recv.at[p, way, s], at_z(z + 1)).wait_send()
        for o in range(1, X):
            remote(dws.at[p, o - 1], dwr.at[p, o - 1], d_send.at[p, o - 1], d_recv.at[p, o - 1], at_x(x)).wait_send()


def solution(mesh):
    Z, Y = mesh.shape["ctx"] // X, mesh.shape["head"] // 2
    H = 2 * Y

    def local(queries, key_vectors, value_vectors, out_grad, out_weight, decay_rate):
        B, C = queries.shape
        D8 = out_grad.shape[1]
        D = out_weight.shape[0]
        CH = D8 // X
        dma = pltpu.SemaphoreType.DMA
        vmem = pltpu.VMEM
        any_spec = pl.BlockSpec(memory_space=pl.ANY)
        return pl.pallas_call(
            functools.partial(kernel, Z, Y),
            out_shape=[jax.ShapeDtypeStruct((B, C), BF16)] * 3 + [jax.ShapeDtypeStruct((CH, C), F32)],
            in_specs=[pl.BlockSpec(memory_space=pltpu.SMEM)] + [any_spec] * 5,
            out_specs=[pl.BlockSpec(memory_space=pltpu.VMEM)] * 4,
            scratch_shapes=[
                vmem((B, C), BF16), vmem((B, C), BF16), vmem((B, C), BF16), vmem((D, C), BF16),
                vmem((H, B, D8), BF16), vmem((Z, B, D8), BF16), vmem((D8, Z * B), BF16),
                vmem((B, C), BF16), vmem((B, C), F32),
                vmem((X, B, B), BF16), vmem((X, B, B), BF16),
                vmem((2, X, E, E), BF16), vmem((2, X, E, E), BF16),
                vmem((2, E, E), BF16), vmem((2, Z, E, E), BF16),
                vmem((2, X, E, E), BF16), vmem((2, X, E, E), BF16), vmem((E, E), F32),
                vmem((2, Z, B, 2 * E), BF16),
                vmem((2, X - 1, CH, 2 * E), BF16), vmem((2, X - 1, CH, 2 * E), BF16),
                dma((5,)), dma((2, 10)), dma((2, 10)), dma((Z,)), dma((Z,)),
                dma((2, X - 1)), dma((2, X - 1)), dma((2, Z - 1)), dma((2, Z - 1)),
                dma((2, X - 1)), dma((2, X - 1)), dma((2, 2, Z // 2)), dma((2, 2, Z // 2)),
                dma((2, X - 1)), dma((2, X - 1)),
            ],
            compiler_params=pltpu.CompilerParams(
                collective_id=0, has_side_effects=True, vmem_limit_bytes=48 * 1024 * 1024),
            name="lightning_backward",
        )(decay_rate, queries, key_vectors, value_vectors, out_grad, out_weight)

    tok = P("ctx", "head")
    return jax.shard_map(
        local, mesh=mesh, in_specs=(tok, tok, tok, tok, P(None, "head"), P("head")),
        out_specs=(tok, tok, tok, tok), check_vma=False)
```

```python
import functools

import jax
import jax.numpy as jnp
from jax import lax
from jax.experimental import pallas as pl
from jax.experimental.pallas import tpu as pltpu
from jax.sharding import PartitionSpec as P

E = 128
X = 4
MESH = pl.DeviceIdType.MESH
F32 = jnp.float32
BF16 = jnp.bfloat16


def dot(a, b, ca=1, cb=0):
    return lax.dot_general(a, b, (((ca,), (cb,)), ((), ())), preferred_element_type=F32)


def kernel(Z, Y, r_hbm, q_hbm, k_hbm, v_hbm, og_hbm, w_hbm, qg_ref, kg_ref, vg_ref, wg_ref,
           r_ref, q, k, v, w, fg, gz, gzt, hg, hacc, sc, gs, ts, tx, rs, rz, ss, st, acc, ab, dws, dwr, fgp,
           local_sem, g_send, g_recv, p_send, p_recv, t_send, t_recv, r_send, r_recv,
           s_send, s_recv, a_send, a_recv, d_send, d_recv, y_send, y_recv):
    B = q.shape[0]
    D8 = fg.shape[2]
    CH = D8 // X
    H = 2 * Y
    PIECE = B // H
    ctx = lax.axis_index("ctx")
    h = lax.axis_index("head")
    z, x = ctx // X, lax.rem(ctx, X)
    y, c = h // 2, lax.rem(h, 2)

    def at_z(zz):
        return (lax.rem(zz + Z, Z) * X + x, h)

    def at_x(xx):
        return (z * X + xx, h)

    def yhead(dy, cc):
        return lax.rem(y + dy + Y, Y) * 2 + cc

    def at_h(hh):
        return (ctx, hh)

    sib = 1 - c

    def remote(src, dst, send, recv, to):
        return pltpu.make_async_remote_copy(
            src_ref=src, dst_ref=dst, send_sem=send, recv_sem=recv, device_id=to, device_id_type=MESH)

    loads = [pltpu.make_async_copy(a, b, local_sem.at[i]) for i, (a, b) in enumerate(
        ((r_hbm, r_ref), (og_hbm, fg.at[h]), (k_hbm, k), (v_hbm, v), (q_hbm, q), (w_hbm, w)))]
    for load in loads:
        load.start()
    barrier = pltpu.get_barrier_semaphore()
    peers = ([at_z(z + d) for d in range(1, Z)] + [at_x(lax.rem(x + o, X)) for o in range(1, X)]
             + [at_h(lax.rem(h + i, H)) for i in range(1, H)])
    for peer in peers:
        pl.semaphore_signal(barrier, inc=1, device_id=peer, device_id_type=MESH)

    rows = lax.broadcasted_iota(jnp.int32, (B, E), 0).astype(F32)
    dist = (lax.broadcasted_iota(jnp.int32, (B, B), 0)
            - lax.broadcasted_iota(jnp.int32, (B, B), 1)).astype(F32)

    def head(ref, j):
        return ref[:, j * E:(j + 1) * E]

    def weights(j):
        return jnp.where(dist >= 0, jnp.exp(-r_ref[j] * jnp.maximum(dist, 0.0)), 0.0)

    def power(rate, count):
        return jnp.exp(jnp.full((1, E), -rate * count, F32))

    def scan_send(g):
        for o in range(1, X):
            peer = lax.rem(x + o, X)
            remote(ts.at[g, peer], tx.at[g, x], t_send.at[g, o - 1], t_recv.at[g, o - 1], at_x(peer)).start()
        tx[g, x] = ts[g, x]

    def scan_rows(g):
        for o in range(1, X):
            src = lax.rem(x - o + X, X)
            remote(ts.at[g, src], tx.at[g, src], t_send.at[g, o - 1], t_recv.at[g, o - 1], at_x(src)).wait_recv()
        total = jnp.zeros((E, E), F32)
        for xx in range(X):
            away = xx if g else X - 1 - xx
            total = total + power(r_own, float(B * away)) * tx[g, xx].astype(F32)
        rs[g] = total.astype(BF16)
        for d in sorted(range(1, Z), key=lambda d: -min(d, Z - d)):
            there = z - d if g else z + d

            @pl.when((there >= 0) & (there < Z))
            def _():
                remote(rs.at[g], rz.at[g, z], r_send.at[g, d - 1], r_recv.at[g, d - 1], at_z(there)).start()

    def scan_finish(g):
        acc[...] = jnp.zeros((E, E), F32)
        for d in range(1, Z):
            src = z + d if g else z - d

            @pl.when((src >= 0) & (src < Z))
            def _():
                remote(rs.at[g], rz.at[g, src], r_send.at[g, d - 1], r_recv.at[g, d - 1], at_z(src)).wait_recv()
                acc[...] += power(r_own, float(X * B * (d - 1))) * rz[g, src].astype(F32)

        state = acc[...]
        step = power(r_own, float(B))
        for xx in (reversed(range(X)) if g else range(X)):
            ss[g, xx] = state.astype(BF16)
            state = step * state + tx[g, xx].astype(F32)
        for o in range(1, X):
            peer = lax.rem(x + o, X)
            remote(ss.at[g, peer], st.at[g, x], s_send.at[g, o - 1], s_recv.at[g, o - 1], at_x(peer)).start()
        st[g, x] = ss[g, x]

    def scan_wait(g):
        for o in range(1, X):
            src = lax.rem(x - o + X, X)
            remote(ss.at[g, src], st.at[g, src], s_send.at[g, o - 1], s_recv.at[g, o - 1], at_x(src)).wait_recv()

    def piece(n, hh, part_at=None):
        if n == 0:
            if part_at is None:
                return fg.at[hh]
            return fg.at[hh, part_at * (B // 4):(part_at + 1) * (B // 4), :]
        mine = pl.ds(pl.multiple_of(hh * PIECE, PIECE), PIECE)
        if part_at is None:
            return gz.at[:, mine, :]
        return gz.at[part_at * (Z // 4):(part_at + 1) * (Z // 4), mine, :]

    def hop(n, hh, part_at, i, to):
        ref = piece(n, hh, part_at)
        return remote(ref, ref, g_send.at[n, i], g_recv.at[n, i], at_h(to))

    up, down = yhead(1, c), yhead(-1, c)
    far = yhead(2, c)
    across = yhead(0, sib)

    def gather_start(n):
        for u, d in ((0, 2), (1, 3)):
            hop(n, h, u, u, up).start()
            hop(n, h, d, 4 + d, down).start()
        hop(n, h, None, 12, across).start()

    def gather_more(n):
        for u, d in ((2, 0), (3, 1)):
            hop(n, h, u, u, up).start()
            hop(n, h, d, 4 + d, down).start()

    def gather_forward(n):
        for u, d in ((0, 2), (1, 3)):
            hop(n, down, u, u, up).wait_recv()
            hop(n, down, u, 8 + u, up).start()
            hop(n, up, d, 4 + d, down).wait_recv()
            hop(n, up, d, 8 + d, down).start()

    def gather_near(n):
        for u, d in ((2, 0), (3, 1)):
            hop(n, down, u, u, up).wait_recv()
            hop(n, up, d, 4 + d, down).wait_recv()
        hop(n, down, None, 13, across).start()
        hop(n, up, None, 14, across).start()

    def gather_far(n):
        for i in range(4):
            hop(n, far, i, 8 + i, up).wait_recv()
        hop(n, far, None, 15, across).start()

    def gather_across(n, i):
        hh = yhead((0, -1, 1, 2)[i], sib)
        hop(n, hh, None, 12 + i, across).wait_recv()
        return hh

    my_piece = pl.ds(pl.multiple_of(h * PIECE, PIECE), PIECE)

    last = Z // 2 - 1

    def ring_copy(p, way, s, block):
        if s > last - 1:
            ref = ab.at[p, block, way * (B // 2):(way + 1) * (B // 2), :]
            there = z - 2 if way else z + 2
        else:
            ref = ab.at[p, block]
            there = z - 1 if way else z + 1
        return remote(ref, ref, a_send.at[p, way, s], a_recv.at[p, way, s], at_z(there))

    def ring(s, p):
        for way in range(2):
            block = lax.rem(z + (s if way else -s) + Z, Z)
            if s > 0:
                ring_copy(p, way, s - 1, block).wait_recv()
            if s < last:
                ring_copy(p, way, s, block).start()
            if s == last - 1:
                ring_copy(p, way, last, block).start()
            if s == last:
                ring_copy(p, way, last, lax.rem(z + Z // 2, Z)).wait_recv()

    places = ((0, sib), (1, c), (1, sib), (-1, c), (-1, sib), (2, c), (2, sib))

    def spread_piece():
        for dy, cc in places:
            hh = yhead(dy, cc)
            remote(fg.at[h, pl.ds(pl.multiple_of(hh * PIECE, PIECE), PIECE), :], fgp.at[h],
                   y_send.at[hh], y_recv.at[h], at_h(hh)).start()
        fgp[h] = fg[h, my_piece, :]

    def pass_piece(zz):
        @pl.when(zz != z)
        def _():
            remote(fgp.at[zz], gz.at[z, my_piece, :], p_send.at[zz], p_recv.at[z], at_z(zz)).start()

        @pl.when(zz == z)
        def _():
            gz[z, my_piece, :] = fgp[zz]

    def pass_pieces():
        for dy, cc in places:
            hh = yhead(dy, cc)
            remote(fgp.at[hh], fgp.at[hh], y_send.at[hh], y_recv.at[hh], at_h(hh)).wait_recv()
            pass_piece(hh)

    for load in loads[:5]:
        load.wait()
    r_own = r_ref[x]
    for j in range(X):
        decayed = (head(k, j).astype(F32) * jnp.exp(-r_ref[j] * (B - 1.0 - rows))).astype(BF16)
        ts[0, j] = dot(decayed, head(v, j), 0, 0).astype(BF16)
    for j in range(X):
        sc[j] = (dot(head(q, j), head(k, j), 1, 1) * weights(j)).astype(BF16)
    pl.semaphore_wait(barrier, len(peers))

    scan_send(0)
    spread_piece()
    gather_start(0)
    pass_piece(h)
    scan_rows(0)
    pass_pieces()
    gather_more(0)
    gather_forward(0)
    gather_near(0)
    scan_finish(0)
    gather_far(0)
    for zz in range(Z):
        @pl.when(zz != z)
        def _():
            remote(gz.at[zz, my_piece, :], gz.at[zz, my_piece, :], p_send.at[zz], p_recv.at[zz], at_z(zz)).wait_recv()
    gather_start(1)
    for i in range(4):
        gather_across(0, i)

    loads[5].wait()
    hacc[...] = jnp.zeros_like(hacc)

    def part(i, carry):
        hacc[...] += dot(fg[i], w[pl.ds(pl.multiple_of(i * D8, D8), D8), :])
        return carry

    lax.fori_loop(0, H, part, 0)
    hg[...] = hacc[...].astype(BF16)
    gather_more(1)

    scan_wait(0)
    for p in range(2):
        for j in (2 * p, 2 * p + 1):
            inter = jnp.exp(-r_ref[j] * (rows + 1.0)) * dot(head(q, j), st[0, j])
            ab[p, z, :, (j % 2) * E:(j % 2 + 1) * E] = (inter + dot(sc[j], head(v, j))).astype(BF16)
        ring(0, p)
    for j in range(X):
        decayed = (head(q, j).astype(F32) * jnp.exp(-r_ref[j] * rows)).astype(BF16)
        ts[1, j] = dot(decayed, head(hg, j), 0, 0).astype(BF16)
    scan_send(1)
    gather_forward(1)
    ring(1, 0)
    ring(1, 1)
    scan_rows(1)
    for j in range(X):
        gs[j] = (dot(head(hg, j), head(v, j), 1, 1) * weights(j)).astype(BF16)
        inter = jnp.exp(-r_ref[j] * (rows + 1.0)) * dot(head(hg, j), st[0, j], 1, 1)
        qg_ref[:, j * E:(j + 1) * E] = (inter + dot(gs[j], head(k, j))).astype(BF16)
    gather_near(1)
    for s in range(2, last):
        ring(s, 0)
        ring(s, 1)
    gather_far(1)
    for i in range(4):
        gather_across(1, i)
    for zz in range(Z):
        gzt[:, zz * B:(zz + 1) * B] = gz[zz].T
    ring(last, 0)
    ring(last, 1)

    def rows_of(xx):
        return gzt[pl.ds(pl.multiple_of(xx * CH, CH), CH), :]

    def partial(p, xx, half):
        at = lax.rem(xx + X, X) * CH + half * (CH // 2)
        return dot(gzt[pl.ds(pl.multiple_of(at, CH // 2), CH // 2), :], ab[p].reshape(Z * B, 2 * E))

    def share(p, way, i):
        return remote(dws.at[p, way, i], dwr.at[p, way, i], d_send.at[p, way, i], d_recv.at[p, way, i],
                      at_x(lax.rem(x + (X - 1 if way else 1), X)))

    for p in range(2):
        for way in range(2):
            dws[p, way, 0] = partial(p, x + 2, way).astype(BF16)
            share(p, way, 0).start()
        for way in range(2):
            dws[p, way, 1] = partial(p, x + (X - 1 if way else 1), 1 - way).astype(BF16)
            share(p, way, 1).start()
    scan_finish(1)
    for p in range(2):
        for way in range(2):
            own = partial(p, x + (X - 1 if way else 1), way)
            share(p, way, 0).wait_recv()
            dws[p, way, 2] = (own + dwr[p, way, 0].astype(F32)).astype(BF16)
            share(p, way, 2).start()
    for p in range(2):
        for half in range(2):
            wg_ref[half * (CH // 2):(half + 1) * (CH // 2), p * 2 * E:(p + 1) * 2 * E] = partial(p, x, half)
    scan_wait(1)
    for j in range(X):
        back = jnp.exp(-r_ref[j] * (B - rows))
        kg_ref[:, j * E:(j + 1) * E] = (
            back * dot(head(v, j), st[1, j], 1, 1) + dot(gs[j], head(q, j), 0, 0)).astype(BF16)
        vg_ref[:, j * E:(j + 1) * E] = (
            back * dot(head(k, j), st[1, j]) + dot(sc[j], head(hg, j), 0, 0)).astype(BF16)
    for i in (1, 2):
        for p in range(2):
            for way in range(2):
                half = 1 - way if i == 1 else way
                share(p, way, i).wait_recv()
                wg_ref[half * (CH // 2):(half + 1) * (CH // 2), p * 2 * E:(p + 1) * 2 * E] += dwr[p, way, i].astype(F32)

    for g in range(2):
        for o in range(1, X):
            remote(ts.at[g, 0], tx.at[g, 0], t_send.at[g, o - 1], t_recv.at[g, o - 1], at_x(x)).wait_send()
            remote(ss.at[g, 0], st.at[g, 0], s_send.at[g, o - 1], s_recv.at[g, o - 1], at_x(x)).wait_send()
        for d in range(1, Z):
            there = z - d if g else z + d

            @pl.when((there >= 0) & (there < Z))
            def _():
                remote(rs.at[g], rz.at[g, z], r_send.at[g, d - 1], r_recv.at[g, d - 1], at_z(there)).wait_send()
    for n in range(2):
        for i, part_at in enumerate((0, 1, 2, 3) * 3 + (None,) * 4):
            hop(n, h, part_at, i, up).wait_send()
    for zz in range(Z):
        @pl.when(zz != z)
        def _():
            remote(fgp.at[zz], gz.at[z, my_piece, :], p_send.at[zz], p_recv.at[z], at_z(zz)).wait_send()
    for dy, cc in places:
        hh = yhead(dy, cc)
        remote(fgp.at[hh], fgp.at[hh], y_send.at[hh], y_recv.at[hh], at_h(hh)).wait_send()
    for p in range(2):
        for way in range(2):
            for s in range(last + 1):
                ring_copy(p, way, s, z).wait_send()
        for way in range(2):
            for i in range(3):
                share(p, way, i).wait_send()


def store(a, b, c, d, a_out, b_out, c_out, d_out, sem):
    copies = [pltpu.make_async_copy(src, dst, sem.at[i]) for i, (src, dst) in enumerate(
        ((d, d_out), (a, a_out), (b, b_out), (c, c_out)))]
    for copy in copies:
        copy.start()
    for copy in copies:
        copy.wait()


def solution(mesh):
    Z, Y = mesh.shape["ctx"] // X, mesh.shape["head"] // 2
    H = 2 * Y

    def local(queries, key_vectors, value_vectors, out_grad, out_weight, decay_rate):
        B, C = queries.shape
        D8 = out_grad.shape[1]
        D = out_weight.shape[0]
        CH = D8 // X
        dma = pltpu.SemaphoreType.DMA
        vmem = pltpu.VMEM
        hbm = pl.BlockSpec(memory_space=pltpu.HBM)
        results = pl.pallas_call(
            functools.partial(kernel, Z, Y),
            out_shape=[jax.ShapeDtypeStruct((B, C), BF16)] * 3 + [jax.ShapeDtypeStruct((CH, C), F32)],
            in_specs=[hbm] * 6,
            out_specs=[pl.BlockSpec(memory_space=pltpu.VMEM)] * 4,
            scratch_shapes=[
                pltpu.SMEM((X,), F32),
                vmem((B, C), BF16), vmem((B, C), BF16), vmem((B, C), BF16), vmem((D, C), BF16),
                vmem((H, B, D8), BF16), vmem((Z, B, D8), BF16), vmem((D8, Z * B), BF16),
                vmem((B, C), BF16), vmem((B, C), F32),
                vmem((X, B, B), BF16), vmem((X, B, B), BF16),
                vmem((2, X, E, E), BF16), vmem((2, X, E, E), BF16),
                vmem((2, E, E), BF16), vmem((2, Z, E, E), BF16),
                vmem((2, X, E, E), BF16), vmem((2, X, E, E), BF16), vmem((E, E), F32),
                vmem((2, Z, B, 2 * E), BF16),
                vmem((2, 2, 3, CH // 2, 2 * E), BF16), vmem((2, 2, 3, CH // 2, 2 * E), BF16),
                vmem((H, B // H, D8), BF16),
                dma((6,)), dma((2, 16)), dma((2, 16)), dma((Z,)), dma((Z,)),
                dma((2, X - 1)), dma((2, X - 1)), dma((2, Z - 1)), dma((2, Z - 1)),
                dma((2, X - 1)), dma((2, X - 1)), dma((2, 2, Z // 2)), dma((2, 2, Z // 2)),
                dma((2, 2, 3)), dma((2, 2, 3)), dma((H,)), dma((H,)),
            ],
            compiler_params=pltpu.CompilerParams(
                collective_id=0, has_side_effects=True, vmem_limit_bytes=63 * 1024 * 1024),
            name="lightning_backward",
        )(decay_rate, queries, key_vectors, value_vectors, out_grad, out_weight)
        return pl.pallas_call(
            store,
            out_shape=[jax.ShapeDtypeStruct(a.shape, a.dtype) for a in results],
            in_specs=[pl.BlockSpec(memory_space=pltpu.VMEM)] * 4,
            out_specs=[hbm] * 4,
            scratch_shapes=[dma((4,))],
            name="store_results",
        )(*results)

    tok = P("ctx", "head")
    return jax.shard_map(
        local, mesh=mesh, in_specs=(tok, tok, tok, tok, P(None, "head"), P("head")),
        out_specs=(tok, tok, tok, tok), check_vma=False)
```

```python
import functools

import jax
import jax.numpy as jnp
from jax import lax
from jax.experimental import pallas as pl
from jax.experimental.pallas import tpu as pltpu
from jax.sharding import PartitionSpec as P

E = 128
X = 4
MESH = pl.DeviceIdType.MESH
F32 = jnp.float32
BF16 = jnp.bfloat16


def dot(a, b, ca=1, cb=0):
    return lax.dot_general(a, b, (((ca,), (cb,)), ((), ())), preferred_element_type=F32)


def kernel(Z, Y, r_hbm, q_hbm, k_hbm, v_hbm, og_hbm, w_hbm, qg_hbm, kg_hbm, vg_hbm, wg_hbm,
           r_ref, q, k, v, w, fg, gz, gzt, hg, hacc, sc, gs, ts, tx, rs, rz, ss, st, acc, ab, dws, dwr, fgp,
           qg_ref, kg_ref, vg_ref, wg_ref, decay, intra,
           local_sem, g_send, g_recv, p_send, p_recv, t_send, t_recv, r_send, r_recv,
           s_send, s_recv, a_send, a_recv, d_send, d_recv, y_send, y_recv, out_sem):
    B = q.shape[0]
    D8 = fg.shape[2]
    CH = D8 // X
    H = 2 * Y
    PIECE = B // H
    ctx = lax.axis_index("ctx")
    h = lax.axis_index("head")
    z, x = ctx // X, lax.rem(ctx, X)
    y, c = h // 2, lax.rem(h, 2)

    def at_z(zz):
        return (lax.rem(zz + Z, Z) * X + x, h)

    def at_x(xx):
        return (z * X + xx, h)

    def yhead(dy, cc):
        return lax.rem(y + dy + Y, Y) * 2 + cc

    def at_h(hh):
        return (ctx, hh)

    sib = 1 - c

    def remote(src, dst, send, recv, to):
        return pltpu.make_async_remote_copy(
            src_ref=src, dst_ref=dst, send_sem=send, recv_sem=recv, device_id=to, device_id_type=MESH)

    loads = [pltpu.make_async_copy(a, b, local_sem.at[i]) for i, (a, b) in enumerate(
        ((r_hbm, r_ref), (og_hbm, fg.at[h]), (k_hbm, k), (v_hbm, v), (q_hbm, q), (w_hbm, w)))]
    for load in loads:
        load.start()
    barrier = pltpu.get_barrier_semaphore()
    peers = ([at_z(z + d) for d in range(1, Z)] + [at_x(lax.rem(x + o, X)) for o in range(1, X)]
             + [at_h(lax.rem(h + i, H)) for i in range(1, H)])
    for peer in peers:
        pl.semaphore_signal(barrier, inc=1, device_id=peer, device_id_type=MESH)

    rows = lax.broadcasted_iota(jnp.int32, (B, E), 0).astype(F32)
    dist = (lax.broadcasted_iota(jnp.int32, (B, B), 0)
            - lax.broadcasted_iota(jnp.int32, (B, B), 1)).astype(F32)

    def head(ref, j):
        return ref[:, j * E:(j + 1) * E]

    def weights(j):
        return jnp.where(dist >= 0, jnp.exp(-r_ref[j] * jnp.maximum(dist, 0.0)), 0.0)

    def power(rate, count):
        return jnp.exp(jnp.full((1, E), -rate * count, F32))

    def scan_send(g):
        for o in range(1, X):
            peer = lax.rem(x + o, X)
            remote(ts.at[g, peer], tx.at[g, x], t_send.at[g, o - 1], t_recv.at[g, o - 1], at_x(peer)).start()
        tx[g, x] = ts[g, x]

    def scan_rows(g):
        for o in range(1, X):
            src = lax.rem(x - o + X, X)
            remote(ts.at[g, src], tx.at[g, src], t_send.at[g, o - 1], t_recv.at[g, o - 1], at_x(src)).wait_recv()
        total = jnp.zeros((E, E), F32)
        for xx in range(X):
            away = xx if g else X - 1 - xx
            total = total + row_power[away] * tx[g, xx].astype(F32)
        rs[g] = total.astype(BF16)
        for d in sorted(range(1, Z), key=lambda d: -min(d, Z - d)):
            there = z - d if g else z + d

            @pl.when((there >= 0) & (there < Z))
            def _():
                remote(rs.at[g], rz.at[g, z], r_send.at[g, d - 1], r_recv.at[g, d - 1], at_z(there)).start()

    def scan_finish(g):
        acc[...] = jnp.zeros((E, E), F32)
        for d in range(1, Z):
            src = z + d if g else z - d

            @pl.when((src >= 0) & (src < Z))
            def _():
                remote(rs.at[g], rz.at[g, src], r_send.at[g, d - 1], r_recv.at[g, d - 1], at_z(src)).wait_recv()
                acc[...] += z_power[d - 1] * rz[g, src].astype(F32)

        state = acc[...]
        for xx in (reversed(range(X)) if g else range(X)):
            ss[g, xx] = state.astype(BF16)
            state = row_power[1] * state + tx[g, xx].astype(F32)
        for o in range(1, X):
            peer = lax.rem(x + o, X)
            remote(ss.at[g, peer], st.at[g, x], s_send.at[g, o - 1], s_recv.at[g, o - 1], at_x(peer)).start()
        st[g, x] = ss[g, x]

    def scan_wait(g):
        for o in range(1, X):
            src = lax.rem(x - o + X, X)
            remote(ss.at[g, src], st.at[g, src], s_send.at[g, o - 1], s_recv.at[g, o - 1], at_x(src)).wait_recv()

    def piece(n, hh, part_at=None):
        if n == 0:
            if part_at is None:
                return fg.at[hh]
            return fg.at[hh, part_at * (B // 4):(part_at + 1) * (B // 4), :]
        mine = pl.ds(pl.multiple_of(hh * PIECE, PIECE), PIECE)
        if part_at is None:
            return gz.at[:, mine, :]
        return gz.at[part_at * (Z // 4):(part_at + 1) * (Z // 4), mine, :]

    def hop(n, hh, part_at, i, to):
        ref = piece(n, hh, part_at)
        return remote(ref, ref, g_send.at[n, i], g_recv.at[n, i], at_h(to))

    up, down = yhead(1, c), yhead(-1, c)
    far = yhead(2, c)
    across = yhead(0, sib)

    def gather_start(n):
        for u, d in ((0, 2), (1, 3)):
            hop(n, h, u, u, up).start()
            hop(n, h, d, 4 + d, down).start()
        hop(n, h, None, 12, across).start()

    def gather_more(n):
        for u, d in ((2, 0), (3, 1)):
            hop(n, h, u, u, up).start()
            hop(n, h, d, 4 + d, down).start()

    def gather_forward(n):
        for u, d in ((0, 2), (1, 3)):
            hop(n, down, u, u, up).wait_recv()
            hop(n, down, u, 8 + u, up).start()
            hop(n, up, d, 4 + d, down).wait_recv()
            hop(n, up, d, 8 + d, down).start()

    def gather_near(n):
        for u, d in ((2, 0), (3, 1)):
            hop(n, down, u, u, up).wait_recv()
            hop(n, up, d, 4 + d, down).wait_recv()
        hop(n, down, None, 13, across).start()
        hop(n, up, None, 14, across).start()

    def gather_far(n):
        for i in range(4):
            hop(n, far, i, 8 + i, up).wait_recv()
        hop(n, far, None, 15, across).start()

    def gather_across(n, i):
        hh = yhead((0, -1, 1, 2)[i], sib)
        hop(n, hh, None, 12 + i, across).wait_recv()
        return hh

    my_piece = pl.ds(pl.multiple_of(h * PIECE, PIECE), PIECE)

    last = Z // 2 - 1

    def ring_copy(p, way, s, block):
        if s > last - 1:
            ref = ab.at[p, block, way * (B // 2):(way + 1) * (B // 2), :]
            there = z - 2 if way else z + 2
        else:
            ref = ab.at[p, block]
            there = z - 1 if way else z + 1
        return remote(ref, ref, a_send.at[p, way, s], a_recv.at[p, way, s], at_z(there))

    def ring(s, p):
        for way in range(2):
            block = lax.rem(z + (s if way else -s) + Z, Z)
            if s > 0:
                ring_copy(p, way, s - 1, block).wait_recv()
            if s < last:
                ring_copy(p, way, s, block).start()
            if s == last - 1:
                ring_copy(p, way, last, block).start()
            if s == last:
                ring_copy(p, way, last, lax.rem(z + Z // 2, Z)).wait_recv()

    places = ((0, sib), (1, c), (1, sib), (-1, c), (-1, sib), (2, c), (2, sib))

    def spread_piece():
        for dy, cc in places:
            hh = yhead(dy, cc)
            remote(fg.at[h, pl.ds(pl.multiple_of(hh * PIECE, PIECE), PIECE), :], fgp.at[h],
                   y_send.at[hh], y_recv.at[h], at_h(hh)).start()
        fgp[h] = fg[h, my_piece, :]

    def pass_piece(zz):
        @pl.when(zz != z)
        def _():
            remote(fgp.at[zz], gz.at[z, my_piece, :], p_send.at[zz], p_recv.at[z], at_z(zz)).start()

        @pl.when(zz == z)
        def _():
            gz[z, my_piece, :] = fgp[zz]

    def pass_pieces():
        for dy, cc in places:
            hh = yhead(dy, cc)
            remote(fgp.at[hh], fgp.at[hh], y_send.at[hh], y_recv.at[hh], at_h(hh)).wait_recv()
            pass_piece(hh)

    for load in loads[:5]:
        load.wait()
    r_own = r_ref[x]
    row_power = [power(r_own, float(B * i)) for i in range(X)]
    z_power = [power(r_own, float(X * B * i)) for i in range(Z - 1)]
    for j in range(X):
        decayed = (head(k, j).astype(F32) * jnp.exp(-r_ref[j] * (B - 1.0 - rows))).astype(BF16)
        ts[0, j] = dot(decayed, head(v, j), 0, 0).astype(BF16)
    for j in range(X):
        sc[j] = (dot(head(q, j), head(k, j), 1, 1) * weights(j)).astype(BF16)
    pl.semaphore_wait(barrier, len(peers))

    def partial(p, xx, half):
        at = lax.rem(xx + X, X) * CH + half * (CH // 2)
        return dot(gzt[pl.ds(pl.multiple_of(at, CH // 2), CH // 2), :], ab[p].reshape(Z * B, 2 * E))

    def share(p, way, i):
        return remote(dws.at[p, way, i], dwr.at[p, way, i], d_send.at[p, way, i], d_recv.at[p, way, i],
                      at_x(lax.rem(x + (X - 1 if way else 1), X)))

    def wait_pieces():
        for zz in range(Z):
            @pl.when(zz != z)
            def _():
                remote(gz.at[zz, my_piece, :], gz.at[zz, my_piece, :], p_send.at[zz], p_recv.at[zz], at_z(zz)).wait_recv()

    def from_sibling(n, *which):
        for i in which:
            gather_across(n, i)

    def head_grad_part(*distances):
        for dy in distances:
            for cc in range(2):
                hh = yhead(dy, cc)
                hacc[...] += dot(fg[hh], w[pl.ds(pl.multiple_of(hh * D8, D8), D8), :])

    def head_grad_start():
        loads[5].wait()
        hacc[...] = jnp.zeros_like(hacc)
        head_grad_part(0)

    def head_grad_end():
        head_grad_part(2)
        hg[...] = hacc[...].astype(BF16)

    def attention_start():
        for j in range(X):
            decay[j] = jnp.exp(-r_ref[j] * (rows + 1.0))
            intra[0, j] = dot(sc[j], head(v, j))

    def attention(p):
        for j in (2 * p, 2 * p + 1):
            inter = decay[j] * dot(head(q, j), st[0, j])
            ab[p, z, :, (j % 2) * E:(j % 2 + 1) * E] = (inter + intra[0, j]).astype(BF16)
        ring(0, p)

    def query_terms():
        for j in range(X):
            decayed = (head(q, j).astype(F32) * jnp.exp(-r_ref[j] * rows)).astype(BF16)
            ts[1, j] = dot(decayed, head(hg, j), 0, 0).astype(BF16)

    def query_grads():
        for j in range(X):
            gs[j] = (dot(head(hg, j), head(v, j), 1, 1) * weights(j)).astype(BF16)
            inter = decay[j] * dot(head(hg, j), st[0, j], 1, 1)
            qg_ref[:, j * E:(j + 1) * E] = (inter + dot(gs[j], head(k, j))).astype(BF16)

    def turn():
        for zz in range(Z):
            gzt[:, zz * B:(zz + 1) * B] = gz[zz].T

    def share_first(p):
        for way in range(2):
            dws[p, way, 0] = partial(p, x + 2, way).astype(BF16)
            share(p, way, 0).start()
        for way in range(2):
            dws[p, way, 1] = partial(p, x + (X - 1 if way else 1), 1 - way).astype(BF16)
            share(p, way, 1).start()

    def share_second(p):
        for way in range(2):
            own = partial(p, x + (X - 1 if way else 1), way)
            share(p, way, 0).wait_recv()
            dws[p, way, 2] = (own + dwr[p, way, 0].astype(F32)).astype(BF16)
            share(p, way, 2).start()

    def share_own():
        for p in range(2):
            for half in range(2):
                wg_ref[half * (CH // 2):(half + 1) * (CH // 2), p * 2 * E:(p + 1) * 2 * E] = partial(p, x, half)

    def key_value_start():
        for j in range(X):
            decay[j] = jnp.exp(-r_ref[j] * (B - rows))
            intra[0, j] = dot(gs[j], head(q, j), 0, 0)
            intra[1, j] = dot(sc[j], head(hg, j), 0, 0)

    def key_value_grads():
        for j in range(X):
            kg_ref[:, j * E:(j + 1) * E] = (
                decay[j] * dot(head(v, j), st[1, j], 1, 1) + intra[0, j]).astype(BF16)
            vg_ref[:, j * E:(j + 1) * E] = (
                decay[j] * dot(head(k, j), st[1, j]) + intra[1, j]).astype(BF16)

    def share_last(i, p):
        for way in range(2):
            half = 1 - way if i == 1 else way
            share(p, way, i).wait_recv()
            wg_ref[half * (CH // 2):(half + 1) * (CH // 2), p * 2 * E:(p + 1) * 2 * E] += dwr[p, way, i].astype(F32)

    def scan_sent(g):
        for o in range(1, X):
            remote(ts.at[g, 0], tx.at[g, 0], t_send.at[g, o - 1], t_recv.at[g, o - 1], at_x(x)).wait_send()
            remote(ss.at[g, 0], st.at[g, 0], s_send.at[g, o - 1], s_recv.at[g, o - 1], at_x(x)).wait_send()
        for d in range(1, Z):
            there = z - d if g else z + d

            @pl.when((there >= 0) & (there < Z))
            def _():
                remote(rs.at[g], rz.at[g, z], r_send.at[g, d - 1], r_recv.at[g, d - 1], at_z(there)).wait_send()

    def gather_sent(n):
        for i, part_at in enumerate((0, 1, 2, 3) * 3 + (None,) * 4):
            hop(n, h, part_at, i, up).wait_send()

    def pieces_sent():
        for zz in range(Z):
            @pl.when(zz != z)
            def _():
                remote(fgp.at[zz], gz.at[z, my_piece, :], p_send.at[zz], p_recv.at[z], at_z(zz)).wait_send()
        for dy, cc in places:
            hh = yhead(dy, cc)
            remote(fgp.at[hh], fgp.at[hh], y_send.at[hh], y_recv.at[hh], at_h(hh)).wait_send()

    def ring_sent():
        for p in range(2):
            for way in range(2):
                for s in range(last + 1):
                    ring_copy(p, way, s, z).wait_send()

    wide = [slice(p * 2 * E, (p + 1) * 2 * E) for p in range(2)]
    outs = [pltpu.make_async_copy(a, b, out_sem.at[i]) for i, (a, b) in enumerate(
        ((qg_ref, qg_hbm), (kg_ref, kg_hbm), (vg_ref, vg_hbm),
         (wg_ref.at[:, wide[0]], wg_hbm.at[:, wide[0]]), (wg_ref.at[:, wide[1]], wg_hbm.at[:, wide[1]])))]

    scan_send(0)
    spread_piece()
    gather_start(0)
    pass_piece(h)
    scan_rows(0)
    attention_start()
    pass_pieces()
    gather_more(0)
    from_sibling(0, 0)
    head_grad_start()
    gather_forward(0)
    gather_near(0)
    scan_finish(0)
    gather_far(0)
    from_sibling(0, 1, 2)
    head_grad_part(1, -1)
    scan_wait(0)
    attention(0)
    attention(1)
    wait_pieces()
    gather_start(1)
    from_sibling(0, 3)
    head_grad_end()
    query_terms()
    scan_send(1)
    gather_more(1)
    ring(1, 0)
    ring(1, 1)
    gather_forward(1)
    query_grads()
    outs[0].start()
    ring(2, 0)
    ring(2, 1)
    gather_near(1)
    scan_rows(1)
    gather_far(1)
    scan_sent(0)
    gather_sent(0)
    key_value_start()
    from_sibling(1, 0, 1, 2, 3)
    turn()
    ring(3, 0)
    ring(3, 1)
    share_first(0)
    share_first(1)
    scan_finish(1)
    share_second(0)
    share_second(1)
    share_own()
    pieces_sent()
    gather_sent(1)
    ring_sent()
    scan_wait(1)
    key_value_grads()
    share_last(1, 0)
    share_last(1, 1)
    outs[1].start()
    outs[2].start()
    share_last(2, 0)
    outs[3].start()
    share_last(2, 1)
    outs[4].start()

    scan_sent(1)
    for p in range(2):
        for way in range(2):
            for i in range(3):
                share(p, way, i).wait_send()
    for copy in outs:
        copy.wait()


def store(*refs):
    results, outs, held, in_sem, out_sem = refs[:4], refs[4:8], refs[8:12], refs[12], refs[13]
    loads = [pltpu.make_async_copy(a, b, in_sem.at[i]) for i, (a, b) in enumerate(zip(results, held))]
    stores = [pltpu.make_async_copy(a, b, out_sem.at[i]) for i, (a, b) in enumerate(zip(held, outs))]
    for load in loads:
        load.start()
    for load, copy in zip(loads, stores):
        load.wait()
        copy.start()
    for copy in stores:
        copy.wait()


def solution(mesh):
    Z, Y = mesh.shape["ctx"] // X, mesh.shape["head"] // 2
    H = 2 * Y

    def local(queries, key_vectors, value_vectors, out_grad, out_weight, decay_rate):
        B, C = queries.shape
        D8 = out_grad.shape[1]
        D = out_weight.shape[0]
        CH = D8 // X
        dma = pltpu.SemaphoreType.DMA
        vmem = pltpu.VMEM
        hbm = pl.BlockSpec(memory_space=pltpu.HBM)
        results = pl.pallas_call(
            functools.partial(kernel, Z, Y),
            out_shape=[jax.ShapeDtypeStruct((B, C), BF16)] * 3 + [jax.ShapeDtypeStruct((CH, C), F32)],
            in_specs=[hbm] * 6,
            out_specs=[hbm] * 4,
            scratch_shapes=[
                pltpu.SMEM((X,), F32),
                vmem((B, C), BF16), vmem((B, C), BF16), vmem((B, C), BF16), vmem((D, C), BF16),
                vmem((H, B, D8), BF16), vmem((Z, B, D8), BF16), vmem((D8, Z * B), BF16),
                vmem((B, C), BF16), vmem((B, C), F32),
                vmem((X, B, B), BF16), vmem((X, B, B), BF16),
                vmem((2, X, E, E), BF16), vmem((2, X, E, E), BF16),
                vmem((2, E, E), BF16), vmem((2, Z, E, E), BF16),
                vmem((2, X, E, E), BF16), vmem((2, X, E, E), BF16), vmem((E, E), F32),
                vmem((2, Z, B, 2 * E), BF16),
                vmem((2, 2, 3, CH // 2, 2 * E), BF16), vmem((2, 2, 3, CH // 2, 2 * E), BF16),
                vmem((H, B // H, D8), BF16),
                vmem((B, C), BF16), vmem((B, C), BF16), vmem((B, C), BF16), vmem((CH, C), F32),
                vmem((X, B, E), F32), vmem((2, X, B, E), F32),
                dma((6,)), dma((2, 16)), dma((2, 16)), dma((Z,)), dma((Z,)),
                dma((2, X - 1)), dma((2, X - 1)), dma((2, Z - 1)), dma((2, Z - 1)),
                dma((2, X - 1)), dma((2, X - 1)), dma((2, 2, Z // 2)), dma((2, 2, Z // 2)),
                dma((2, 2, 3)), dma((2, 2, 3)), dma((H,)), dma((H,)), dma((5,)),
            ],
            compiler_params=pltpu.CompilerParams(
                collective_id=0, has_side_effects=True, vmem_limit_bytes=63 * 1024 * 1024),
            name="lightning_backward",
        )(decay_rate, queries, key_vectors, value_vectors, out_grad, out_weight)
        return pl.pallas_call(
            store,
            out_shape=[jax.ShapeDtypeStruct(a.shape, a.dtype) for a in results],
            in_specs=[hbm] * 4,
            out_specs=[hbm] * 4,
            scratch_shapes=[vmem(a.shape, a.dtype) for a in results] + [dma((4,)), dma((4,))],
            compiler_params=pltpu.CompilerParams(vmem_limit_bytes=63 * 1024 * 1024),
            name="store_results",
        )(*results)

    tok = P("ctx", "head")
    return jax.shard_map(
        local, mesh=mesh, in_specs=(tok, tok, tok, tok, P(None, "head"), P("head")),
        out_specs=(tok, tok, tok, tok), check_vma=False)
```

```python
import functools

import jax
import jax.numpy as jnp
from jax import lax
from jax.experimental import pallas as pl
from jax.experimental.pallas import tpu as pltpu
from jax.sharding import PartitionSpec as P

E = 128
X = 4
MESH = pl.DeviceIdType.MESH
F32 = jnp.float32
BF16 = jnp.bfloat16


def dot(a, b, ca=1, cb=0):
    return lax.dot_general(a, b, (((ca,), (cb,)), ((), ())), preferred_element_type=F32)


def kernel(Z, Y, r_hbm, q_hbm, k_hbm, v_hbm, og_hbm, w_hbm, qg_hbm, kg_hbm, vg_hbm, wg_hbm,
           r_ref, q, k, v, w, fg, gz, gzt, hg, hacc, sc, gs, ts, tx, rs, rz, ss, st, acc, ab, dws, dwr, fgp,
           qg_ref, kg_ref, vg_ref, wg_ref, decay, intra,
           local_sem, g_send, g_recv, p_send, p_recv, t_send, t_recv, r_send, r_recv,
           s_send, s_recv, a_send, a_recv, d_send, d_recv, y_send, y_recv, out_sem):
    B = q.shape[0]
    D8 = fg.shape[2]
    CH = D8 // X
    H = 2 * Y
    PIECE = B // H
    ctx = lax.axis_index("ctx")
    h = lax.axis_index("head")
    z, x = ctx // X, lax.rem(ctx, X)
    y, c = h // 2, lax.rem(h, 2)

    def at_z(zz):
        return (lax.rem(zz + Z, Z) * X + x, h)

    def at_x(xx):
        return (z * X + xx, h)

    def yhead(dy, cc):
        return lax.rem(y + dy + Y, Y) * 2 + cc

    def at_h(hh):
        return (ctx, hh)

    sib = 1 - c
    half = Z // 2

    def remote(src, dst, send, recv, to):
        return pltpu.make_async_remote_copy(
            src_ref=src, dst_ref=dst, send_sem=send, recv_sem=recv, device_id=to, device_id_type=MESH)

    loads = [pltpu.make_async_copy(a, b, local_sem.at[i]) for i, (a, b) in enumerate(
        ((r_hbm, r_ref), (k_hbm, k), (v_hbm, v), (og_hbm, fg.at[h]), (q_hbm, q), (w_hbm, w)))]
    for load in loads:
        load.start()
    barrier = pltpu.get_barrier_semaphore()
    peers = ([at_z(z + d) for d in range(1, Z)] + [at_x(lax.rem(x + o, X)) for o in range(1, X)]
             + [at_h(lax.rem(h + i, H)) for i in range(1, H)])
    for peer in peers:
        pl.semaphore_signal(barrier, inc=1, device_id=peer, device_id_type=MESH)

    rows = lax.broadcasted_iota(jnp.int32, (B, E), 0).astype(F32)
    dist = (lax.broadcasted_iota(jnp.int32, (B, B), 0)
            - lax.broadcasted_iota(jnp.int32, (B, B), 1)).astype(F32)

    def head(ref, j):
        return ref[:, j * E:(j + 1) * E]

    def weights(j):
        return jnp.where(dist >= 0, jnp.exp(-r_ref[j] * jnp.maximum(dist, 0.0)), 0.0)

    def power(rate, count):
        return jnp.exp(jnp.full((1, E), -rate * count, F32))

    def scan_send(g):
        for o in range(1, X):
            peer = lax.rem(x + o, X)
            remote(ts.at[g, peer], tx.at[g, x], t_send.at[g, o - 1], t_recv.at[g, o - 1], at_x(peer)).start()
        tx[g, x] = ts[g, x]

    def scan_rows(g):
        for o in range(1, X):
            src = lax.rem(x - o + X, X)
            remote(ts.at[g, src], tx.at[g, src], t_send.at[g, o - 1], t_recv.at[g, o - 1], at_x(src)).wait_recv()
        total = jnp.zeros((E, E), F32)
        for xx in range(X):
            away = xx if g else X - 1 - xx
            total = total + row_power[away] * tx[g, xx].astype(F32)
        rs[g] = total.astype(BF16)
        for d in sorted(range(1, Z), key=lambda d: -min(d, Z - d)):
            there = z - d if g else z + d
            now = (there // half == z // half) if g else True

            @pl.when((there >= 0) & (there < Z) & now)
            def _():
                send_row(g, d, there)

    def send_row(g, d, there):
        remote(rs.at[g], rz.at[g, z], r_send.at[g, d - 1], r_recv.at[g, d - 1], at_z(there)).start()

    def add_row(g, d, src):
        remote(rs.at[g], rz.at[g, src], r_send.at[g, d - 1], r_recv.at[g, d - 1], at_z(src)).wait_recv()
        acc[...] += z_power[d - 1] * rz[g, src].astype(F32)

    def scan_mid(g):
        acc[...] = jnp.zeros((E, E), F32)

        @pl.when(z == half)
        def _():
            for d in range(1, Z - half):
                add_row(g, d, z + d)
            rs[g] = (rs[g].astype(F32) + z_power[1] * acc[...]).astype(BF16)
            for d in range(half, 0, -1):
                send_row(g, d, z - d)

    def scan_finish(g):
        if g == 0:
            acc[...] = jnp.zeros((E, E), F32)
        for d in range(1, Z):
            src = z + d if g else z - d
            now = ((src // half == z // half) | (src == half)) & (z != half) if g else True

            @pl.when((src >= 0) & (src < Z) & now)
            def _():
                add_row(g, d, src)

        state = acc[...]
        for xx in (reversed(range(X)) if g else range(X)):
            ss[g, xx] = state.astype(BF16)
            state = row_power[1] * state + tx[g, xx].astype(F32)
        for o in range(1, X):
            peer = lax.rem(x + o, X)
            remote(ss.at[g, peer], st.at[g, x], s_send.at[g, o - 1], s_recv.at[g, o - 1], at_x(peer)).start()
        st[g, x] = ss[g, x]

    def scan_wait(g):
        for o in range(1, X):
            src = lax.rem(x - o + X, X)
            remote(ss.at[g, src], st.at[g, src], s_send.at[g, o - 1], s_recv.at[g, o - 1], at_x(src)).wait_recv()

    def piece(n, hh, part_at=None):
        if n == 0:
            if part_at is None:
                return fg.at[hh]
            return fg.at[hh, part_at * (B // 4):(part_at + 1) * (B // 4), :]
        mine = pl.ds(pl.multiple_of(hh * PIECE, PIECE), PIECE)
        if part_at is None:
            return gz.at[:, mine, :]
        return gz.at[part_at * (Z // 4):(part_at + 1) * (Z // 4), mine, :]

    def hop(n, hh, part_at, i, to):
        ref = piece(n, hh, part_at)
        return remote(ref, ref, g_send.at[n, i], g_recv.at[n, i], at_h(to))

    up, down = yhead(1, c), yhead(-1, c)
    far = yhead(2, c)
    across = yhead(0, sib)

    def gather_start(n):
        for u, d in ((0, 2), (1, 3)):
            hop(n, h, u, u, up).start()
            hop(n, h, d, 4 + d, down).start()
        hop(n, h, None, 12, across).start()

    def gather_more(n):
        for u, d in ((2, 0), (3, 1)):
            hop(n, h, u, u, up).start()
            hop(n, h, d, 4 + d, down).start()

    def gather_forward(n):
        for u, d in ((0, 2), (1, 3)):
            hop(n, down, u, u, up).wait_recv()
            hop(n, down, u, 8 + u, up).start()
            hop(n, up, d, 4 + d, down).wait_recv()
            hop(n, up, d, 8 + d, down).start()

    def gather_near(n):
        for u, d in ((2, 0), (3, 1)):
            hop(n, down, u, u, up).wait_recv()
            hop(n, up, d, 4 + d, down).wait_recv()
        hop(n, down, None, 13, across).start()
        hop(n, up, None, 14, across).start()

    def gather_far(n):
        for i in range(4):
            hop(n, far, i, 8 + i, up).wait_recv()
        hop(n, far, None, 15, across).start()

    def gather_across(n, i):
        hh = yhead((0, -1, 1, 2)[i], sib)
        hop(n, hh, None, 12 + i, across).wait_recv()
        return hh

    my_piece = pl.ds(pl.multiple_of(h * PIECE, PIECE), PIECE)

    last = Z // 2 - 1

    def ring_copy(p, way, s, block):
        if s > last - 1:
            ref = ab.at[p, block, way * (B // 2):(way + 1) * (B // 2), :]
            there = z - 2 if way else z + 2
        else:
            ref = ab.at[p, block]
            there = z - 1 if way else z + 1
        return remote(ref, ref, a_send.at[p, way, s], a_recv.at[p, way, s], at_z(there))

    def ring(s, p):
        for way in range(2):
            block = lax.rem(z + (s if way else -s) + Z, Z)
            if s > 0:
                ring_copy(p, way, s - 1, block).wait_recv()
            if s < last:
                ring_copy(p, way, s, block).start()
            if s == last - 1:
                ring_copy(p, way, last, block).start()
            if s == last:
                ring_copy(p, way, last, lax.rem(z + Z // 2, Z)).wait_recv()

    places = ((0, sib), (1, c), (1, sib), (-1, c), (-1, sib), (2, c), (2, sib))

    def spread_piece():
        for dy, cc in places:
            hh = yhead(dy, cc)
            remote(fg.at[h, pl.ds(pl.multiple_of(hh * PIECE, PIECE), PIECE), :], fgp.at[h],
                   y_send.at[hh], y_recv.at[h], at_h(hh)).start()
        fgp[h] = fg[h, my_piece, :]

    def pass_piece(zz):
        @pl.when(zz != z)
        def _():
            remote(fgp.at[zz], gz.at[z, my_piece, :], p_send.at[zz], p_recv.at[z], at_z(zz)).start()

        @pl.when(zz == z)
        def _():
            gz[z, my_piece, :] = fgp[zz]

    def pass_pieces():
        for dy, cc in places:
            hh = yhead(dy, cc)
            remote(fgp.at[hh], fgp.at[hh], y_send.at[hh], y_recv.at[hh], at_h(hh)).wait_recv()
            pass_piece(hh)

    for load in loads[:4]:
        load.wait()
    r_own = r_ref[x]
    row_power = [power(r_own, float(B * i)) for i in range(X)]
    z_power = [power(r_own, float(X * B * i)) for i in range(Z - 1)]
    for j in range(X):
        decayed = (head(k, j).astype(F32) * jnp.exp(-r_ref[j] * (B - 1.0 - rows))).astype(BF16)
        ts[0, j] = dot(decayed, head(v, j), 0, 0).astype(BF16)
    pl.semaphore_wait(barrier, len(peers))

    def partial(p, xx, part_at):
        at = lax.rem(xx + X, X) * CH + part_at * (CH // 2)
        return dot(gzt[pl.ds(pl.multiple_of(at, CH // 2), CH // 2), :], ab[p].reshape(Z * B, 2 * E))

    def share(p, way, i):
        return remote(dws.at[p, way, i], dwr.at[p, way, i], d_send.at[p, way, i], d_recv.at[p, way, i],
                      at_x(lax.rem(x + (X - 1 if way else 1), X)))

    def wait_pieces():
        for zz in range(Z):
            @pl.when(zz != z)
            def _():
                remote(gz.at[zz, my_piece, :], gz.at[zz, my_piece, :], p_send.at[zz], p_recv.at[zz], at_z(zz)).wait_recv()

    def from_sibling(n, *which):
        for i in which:
            gather_across(n, i)

    def head_grad_part(*distances):
        for dy in distances:
            for cc in range(2):
                hh = yhead(dy, cc)
                hacc[...] += dot(fg[hh], w[pl.ds(pl.multiple_of(hh * D8, D8), D8), :])

    def head_grad_start():
        loads[5].wait()
        hacc[...] = jnp.zeros_like(hacc)
        head_grad_part(0)

    def head_grad_end():
        head_grad_part(2)
        hg[...] = hacc[...].astype(BF16)

    def attention_scores():
        loads[4].wait()
        for j in range(X):
            sc[j] = (dot(head(q, j), head(k, j), 1, 1) * weights(j)).astype(BF16)

    def attention_start():
        for j in range(X):
            decay[j] = jnp.exp(-r_ref[j] * (rows + 1.0))
            intra[0, j] = dot(sc[j], head(v, j))

    def attention(p):
        for j in (2 * p, 2 * p + 1):
            inter = decay[j] * dot(head(q, j), st[0, j])
            ab[p, z, :, (j % 2) * E:(j % 2 + 1) * E] = (inter + intra[0, j]).astype(BF16)
        ring(0, p)

    def query_terms():
        for j in range(X):
            decayed = (head(q, j).astype(F32) * jnp.exp(-r_ref[j] * rows)).astype(BF16)
            ts[1, j] = dot(decayed, head(hg, j), 0, 0).astype(BF16)

    def query_grads():
        for j in range(X):
            gs[j] = (dot(head(hg, j), head(v, j), 1, 1) * weights(j)).astype(BF16)
            inter = decay[j] * dot(head(hg, j), st[0, j], 1, 1)
            qg_ref[:, j * E:(j + 1) * E] = (inter + dot(gs[j], head(k, j))).astype(BF16)

    def turn():
        for zz in range(Z):
            gzt[:, zz * B:(zz + 1) * B] = gz[zz].T

    def share_first(p):
        for way in range(2):
            dws[p, way, 0] = partial(p, x + 2, way).astype(BF16)
            share(p, way, 0).start()

    def share_direct(p):
        for way in range(2):
            dws[p, way, 1] = partial(p, x + (X - 1 if way else 1), 1 - way).astype(BF16)
            share(p, way, 1).start()

    def share_second(p):
        for way in range(2):
            own = partial(p, x + (X - 1 if way else 1), way)
            share(p, way, 0).wait_recv()
            dws[p, way, 2] = (own + dwr[p, way, 0].astype(F32)).astype(BF16)
            share(p, way, 2).start()

    def share_own():
        for p in range(2):
            for part_at in range(2):
                wg_ref[part_at * (CH // 2):(part_at + 1) * (CH // 2), p * 2 * E:(p + 1) * 2 * E] = partial(p, x, part_at)

    def key_value_start():
        for j in range(X):
            decay[j] = jnp.exp(-r_ref[j] * (B - rows))
            intra[0, j] = dot(gs[j], head(q, j), 0, 0)
            intra[1, j] = dot(sc[j], head(hg, j), 0, 0)

    def key_value_grads():
        for j in range(X):
            kg_ref[:, j * E:(j + 1) * E] = (
                decay[j] * dot(head(v, j), st[1, j], 1, 1) + intra[0, j]).astype(BF16)
            vg_ref[:, j * E:(j + 1) * E] = (
                decay[j] * dot(head(k, j), st[1, j]) + intra[1, j]).astype(BF16)

    def share_last(i, p):
        for way in range(2):
            part_at = 1 - way if i == 1 else way
            share(p, way, i).wait_recv()
            wg_ref[part_at * (CH // 2):(part_at + 1) * (CH // 2), p * 2 * E:(p + 1) * 2 * E] += dwr[p, way, i].astype(F32)

    def scan_sent(g):
        for o in range(1, X):
            remote(ts.at[g, 0], tx.at[g, 0], t_send.at[g, o - 1], t_recv.at[g, o - 1], at_x(x)).wait_send()
            remote(ss.at[g, 0], st.at[g, 0], s_send.at[g, o - 1], s_recv.at[g, o - 1], at_x(x)).wait_send()
        for d in range(1, Z):
            there = z - d if g else z + d
            ever = (there // half == z // half) | (z == half) if g else True

            @pl.when((there >= 0) & (there < Z) & ever)
            def _():
                remote(rs.at[g], rz.at[g, z], r_send.at[g, d - 1], r_recv.at[g, d - 1], at_z(there)).wait_send()

    def gather_sent(n):
        for i, part_at in enumerate((0, 1, 2, 3) * 3 + (None,) * 4):
            hop(n, h, part_at, i, up).wait_send()

    def pieces_sent():
        for zz in range(Z):
            @pl.when(zz != z)
            def _():
                remote(fgp.at[zz], gz.at[z, my_piece, :], p_send.at[zz], p_recv.at[z], at_z(zz)).wait_send()
        for dy, cc in places:
            hh = yhead(dy, cc)
            remote(fgp.at[hh], fgp.at[hh], y_send.at[hh], y_recv.at[hh], at_h(hh)).wait_send()

    def ring_sent():
        for p in range(2):
            for way in range(2):
                for s in range(last + 1):
                    ring_copy(p, way, s, z).wait_send()

    wide = [slice(p * 2 * E, (p + 1) * 2 * E) for p in range(2)]
    outs = [pltpu.make_async_copy(a, b, out_sem.at[i]) for i, (a, b) in enumerate(
        ((qg_ref, qg_hbm), (kg_ref, kg_hbm), (vg_ref, vg_hbm),
         (wg_ref.at[:, wide[0]], wg_hbm.at[:, wide[0]]), (wg_ref.at[:, wide[1]], wg_hbm.at[:, wide[1]])))]

    scan_send(0)
    spread_piece()
    gather_start(0)
    pass_piece(h)
    attention_scores()
    scan_rows(0)
    attention_start()
    gather_more(0)
    from_sibling(0, 0)
    head_grad_start()
    gather_forward(0)
    pass_pieces()
    gather_near(0)
    scan_finish(0)
    gather_far(0)
    from_sibling(0, 1, 2)
    head_grad_part(1, -1)
    scan_wait(0)
    attention(0)
    attention(1)
    wait_pieces()
    gather_start(1)
    from_sibling(0, 3)
    head_grad_end()
    query_terms()
    scan_send(1)
    gather_more(1)
    ring(1, 0)
    ring(1, 1)
    gather_forward(1)
    scan_rows(1)
    query_grads()
    outs[0].start()
    ring(2, 0)
    ring(2, 1)
    gather_near(1)
    scan_mid(1)
    gather_far(1)
    scan_sent(0)
    gather_sent(0)
    key_value_start()
    from_sibling(1, 0, 1, 2, 3)
    turn()
    ring(3, 0)
    share_first(0)
    ring(3, 1)
    share_first(1)
    share_direct(0)
    share_direct(1)
    scan_finish(1)
    share_second(0)
    share_second(1)
    share_own()
    pieces_sent()
    gather_sent(1)
    ring_sent()
    scan_wait(1)
    key_value_grads()
    share_last(1, 0)
    share_last(1, 1)
    outs[1].start()
    outs[2].start()
    share_last(2, 0)
    outs[3].start()
    share_last(2, 1)
    outs[4].start()

    scan_sent(1)
    for p in range(2):
        for way in range(2):
            for i in range(3):
                share(p, way, i).wait_send()
    for copy in outs:
        copy.wait()


def store(*refs):
    results, outs, held, in_sem, out_sem = refs[:4], refs[4:8], refs[8:12], refs[12], refs[13]
    loads = [pltpu.make_async_copy(a, b, in_sem.at[i]) for i, (a, b) in enumerate(zip(results, held))]
    stores = [pltpu.make_async_copy(a, b, out_sem.at[i]) for i, (a, b) in enumerate(zip(held, outs))]
    for load in loads:
        load.start()
    for load, copy in zip(loads, stores):
        load.wait()
        copy.start()
    for copy in stores:
        copy.wait()


def solution(mesh):
    Z, Y = mesh.shape["ctx"] // X, mesh.shape["head"] // 2
    H = 2 * Y

    def local(queries, key_vectors, value_vectors, out_grad, out_weight, decay_rate):
        B, C = queries.shape
        D8 = out_grad.shape[1]
        D = out_weight.shape[0]
        CH = D8 // X
        dma = pltpu.SemaphoreType.DMA
        vmem = pltpu.VMEM
        hbm = pl.BlockSpec(memory_space=pltpu.HBM)
        results = pl.pallas_call(
            functools.partial(kernel, Z, Y),
            out_shape=[jax.ShapeDtypeStruct((B, C), BF16)] * 3 + [jax.ShapeDtypeStruct((CH, C), F32)],
            in_specs=[hbm] * 6,
            out_specs=[hbm] * 4,
            scratch_shapes=[
                pltpu.SMEM((X,), F32),
                vmem((B, C), BF16), vmem((B, C), BF16), vmem((B, C), BF16), vmem((D, C), BF16),
                vmem((H, B, D8), BF16), vmem((Z, B, D8), BF16), vmem((D8, Z * B), BF16),
                vmem((B, C), BF16), vmem((B, C), F32),
                vmem((X, B, B), BF16), vmem((X, B, B), BF16),
                vmem((2, X, E, E), BF16), vmem((2, X, E, E), BF16),
                vmem((2, E, E), BF16), vmem((2, Z, E, E), BF16),
                vmem((2, X, E, E), BF16), vmem((2, X, E, E), BF16), vmem((E, E), F32),
                vmem((2, Z, B, 2 * E), BF16),
                vmem((2, 2, 3, CH // 2, 2 * E), BF16), vmem((2, 2, 3, CH // 2, 2 * E), BF16),
                vmem((H, B // H, D8), BF16),
                vmem((B, C), BF16), vmem((B, C), BF16), vmem((B, C), BF16), vmem((CH, C), F32),
                vmem((X, B, E), F32), vmem((2, X, B, E), F32),
                dma((6,)), dma((2, 16)), dma((2, 16)), dma((Z,)), dma((Z,)),
                dma((2, X - 1)), dma((2, X - 1)), dma((2, Z - 1)), dma((2, Z - 1)),
                dma((2, X - 1)), dma((2, X - 1)), dma((2, 2, Z // 2)), dma((2, 2, Z // 2)),
                dma((2, 2, 3)), dma((2, 2, 3)), dma((H,)), dma((H,)), dma((5,)),
            ],
            compiler_params=pltpu.CompilerParams(
                collective_id=0, has_side_effects=True, vmem_limit_bytes=63 * 1024 * 1024),
            name="lightning_backward",
        )(decay_rate, queries, key_vectors, value_vectors, out_grad, out_weight)
        return pl.pallas_call(
            store,
            out_shape=[jax.ShapeDtypeStruct(a.shape, a.dtype) for a in results],
            in_specs=[hbm] * 4,
            out_specs=[hbm] * 4,
            scratch_shapes=[vmem(a.shape, a.dtype) for a in results] + [dma((4,)), dma((4,))],
            compiler_params=pltpu.CompilerParams(vmem_limit_bytes=63 * 1024 * 1024),
            name="store_results",
        )(*results)

    tok = P("ctx", "head")
    return jax.shard_map(
        local, mesh=mesh, in_specs=(tok, tok, tok, tok, P(None, "head"), P("head")),
        out_specs=(tok, tok, tok, tok), check_vma=False)
```

```python
import functools

import jax
import jax.numpy as jnp
from jax import lax
from jax.experimental import pallas as pl
from jax.experimental.pallas import tpu as pltpu
from jax.sharding import PartitionSpec as P

E = 128
X = 4
MESH = pl.DeviceIdType.MESH
F32 = jnp.float32
BF16 = jnp.bfloat16


def dot(a, b, ca=1, cb=0):
    return lax.dot_general(a, b, (((ca,), (cb,)), ((), ())), preferred_element_type=F32)


def kernel(Z, Y, r_hbm, q_hbm, k_hbm, v_hbm, og_hbm, w_hbm, qg_hbm, kg_hbm, vg_hbm, wg_hbm,
           r_ref, q, k, v, w, fg, gz, gzt, hg, hacc, sc, gs, ts, tx, rs, rz, ss, st, acc, ab, dws, dwr, fgp,
           qg_ref, kg_ref, vg_ref, wg_ref, decay, intra,
           local_sem, g_send, g_recv, p_send, p_recv, t_send, t_recv, r_send, r_recv,
           s_send, s_recv, a_send, a_recv, d_send, d_recv, y_send, y_recv, out_sem):
    B = q.shape[0]
    D8 = fg.shape[2]
    CH = D8 // X
    H = 2 * Y
    PIECE = B // H
    ctx = lax.axis_index("ctx")
    h = lax.axis_index("head")
    z, x = ctx // X, lax.rem(ctx, X)
    y, c = h // 2, lax.rem(h, 2)

    def at_z(zz):
        return (lax.rem(zz + Z, Z) * X + x, h)

    def at_x(xx):
        return (z * X + xx, h)

    def yhead(dy, cc):
        return lax.rem(y + dy + Y, Y) * 2 + cc

    def at_h(hh):
        return (ctx, hh)

    sib = 1 - c
    half = Z // 2

    def remote(src, dst, send, recv, to):
        return pltpu.make_async_remote_copy(
            src_ref=src, dst_ref=dst, send_sem=send, recv_sem=recv, device_id=to, device_id_type=MESH)

    loads = [pltpu.make_async_copy(a, b, local_sem.at[i]) for i, (a, b) in enumerate(
        ((r_hbm, r_ref), (k_hbm, k), (v_hbm, v), (og_hbm, fg.at[h]), (q_hbm, q), (w_hbm, w)))]
    for load in loads:
        load.start()
    barrier = pltpu.get_barrier_semaphore()
    peers = ([at_z(z + d) for d in range(1, Z)] + [at_x(lax.rem(x + o, X)) for o in range(1, X)]
             + [at_h(lax.rem(h + i, H)) for i in range(1, H)])
    for peer in peers:
        pl.semaphore_signal(barrier, inc=1, device_id=peer, device_id_type=MESH)

    rows = lax.broadcasted_iota(jnp.int32, (B, E), 0).astype(F32)
    dist = (lax.broadcasted_iota(jnp.int32, (B, B), 0)
            - lax.broadcasted_iota(jnp.int32, (B, B), 1)).astype(F32)

    def head(ref, j):
        return ref[:, j * E:(j + 1) * E]

    def weights(j):
        return jnp.where(dist >= 0, jnp.exp(-r_ref[j] * jnp.maximum(dist, 0.0)), 0.0)

    def power(rate, count):
        return jnp.exp(jnp.full((1, E), -rate * count, F32))

    def scan_send(g):
        for o in range(1, X):
            peer = lax.rem(x + o, X)
            remote(ts.at[g, peer], tx.at[g, x], t_send.at[g, o - 1], t_recv.at[g, o - 1], at_x(peer)).start()
        tx[g, x] = ts[g, x]

    def scan_rows(g):
        for o in range(1, X):
            src = lax.rem(x - o + X, X)
            remote(ts.at[g, src], tx.at[g, src], t_send.at[g, o - 1], t_recv.at[g, o - 1], at_x(src)).wait_recv()
        total = jnp.zeros((E, E), F32)
        for xx in range(X):
            away = xx if g else X - 1 - xx
            total = total + row_power[away] * tx[g, xx].astype(F32)
        rs[g] = total.astype(BF16)
        for d in sorted(range(1, Z), key=lambda d: -min(d, Z - d)):
            there = z - d if g else z + d
            now = (there // half == z // half) if g else True

            @pl.when((there >= 0) & (there < Z) & now)
            def _():
                send_row(g, d, there)

    def send_row(g, d, there):
        remote(rs.at[g], rz.at[g, z], r_send.at[g, d - 1], r_recv.at[g, d - 1], at_z(there)).start()

    def add_row(g, d, src):
        remote(rs.at[g], rz.at[g, src], r_send.at[g, d - 1], r_recv.at[g, d - 1], at_z(src)).wait_recv()
        acc[...] += z_power[d - 1] * rz[g, src].astype(F32)

    def scan_mid(g):
        acc[...] = jnp.zeros((E, E), F32)

        @pl.when(z == half)
        def _():
            for d in range(1, Z - half):
                add_row(g, d, z + d)
            rs[g] = (rs[g].astype(F32) + z_power[1] * acc[...]).astype(BF16)
            for d in range(half, 0, -1):
                send_row(g, d, z - d)

    def scan_finish(g):
        if g == 0:
            acc[...] = jnp.zeros((E, E), F32)
        for d in range(1, Z):
            src = z + d if g else z - d
            now = ((src // half == z // half) | (src == half)) & (z != half) if g else True

            @pl.when((src >= 0) & (src < Z) & now)
            def _():
                add_row(g, d, src)

        state = acc[...]
        for xx in (reversed(range(X)) if g else range(X)):
            ss[g, xx] = state.astype(BF16)
            state = row_power[1] * state + tx[g, xx].astype(F32)
        for o in range(1, X):
            peer = lax.rem(x + o, X)
            remote(ss.at[g, peer], st.at[g, x], s_send.at[g, o - 1], s_recv.at[g, o - 1], at_x(peer)).start()
        st[g, x] = ss[g, x]

    def scan_wait(g):
        for o in range(1, X):
            src = lax.rem(x - o + X, X)
            remote(ss.at[g, src], st.at[g, src], s_send.at[g, o - 1], s_recv.at[g, o - 1], at_x(src)).wait_recv()

    def piece(n, hh, part_at=None):
        if n == 0:
            if part_at is None:
                return fg.at[hh]
            return fg.at[hh, part_at * (B // 4):(part_at + 1) * (B // 4), :]
        mine = pl.ds(pl.multiple_of(hh * PIECE, PIECE), PIECE)
        if part_at is None:
            return gz.at[:, mine, :]
        return gz.at[part_at * (Z // 4):(part_at + 1) * (Z // 4), mine, :]

    def hop(n, hh, part_at, i, to):
        ref = piece(n, hh, part_at)
        return remote(ref, ref, g_send.at[n, i], g_recv.at[n, i], at_h(to))

    up, down = yhead(1, c), yhead(-1, c)
    far = yhead(2, c)
    across = yhead(0, sib)

    def gather_start(n):
        for u, d in ((0, 2), (1, 3)):
            hop(n, h, u, u, up).start()
            hop(n, h, d, 4 + d, down).start()
        hop(n, h, None, 12, across).start()

    def gather_more(n):
        for u, d in ((2, 0), (3, 1)):
            hop(n, h, u, u, up).start()
            hop(n, h, d, 4 + d, down).start()

    def gather_forward(n):
        for u, d in ((0, 2), (1, 3)):
            hop(n, down, u, u, up).wait_recv()
            hop(n, down, u, 8 + u, up).start()
            hop(n, up, d, 4 + d, down).wait_recv()
            hop(n, up, d, 8 + d, down).start()

    def gather_near(n):
        for u, d in ((2, 0), (3, 1)):
            hop(n, down, u, u, up).wait_recv()
            hop(n, up, d, 4 + d, down).wait_recv()
        hop(n, down, None, 13, across).start()
        hop(n, up, None, 14, across).start()

    def gather_far(n):
        for i in range(4):
            hop(n, far, i, 8 + i, up).wait_recv()
        hop(n, far, None, 15, across).start()

    def gather_across(n, i):
        hh = yhead((0, -1, 1, 2)[i], sib)
        hop(n, hh, None, 12 + i, across).wait_recv()
        return hh

    my_piece = pl.ds(pl.multiple_of(h * PIECE, PIECE), PIECE)

    last = Z // 2 - 1

    def ring_copy(p, way, s, block):
        if s > last - 1:
            ref = ab.at[p, block, way * (B // 2):(way + 1) * (B // 2), :]
            there = z - 2 if way else z + 2
        else:
            ref = ab.at[p, block]
            there = z - 1 if way else z + 1
        return remote(ref, ref, a_send.at[p, way, s], a_recv.at[p, way, s], at_z(there))

    def ring(s, p):
        for way in range(2):
            block = lax.rem(z + (s if way else -s) + Z, Z)
            if s > 0:
                ring_copy(p, way, s - 1, block).wait_recv()
            if s < last:
                ring_copy(p, way, s, block).start()
            if s == last - 1:
                ring_copy(p, way, last, block).start()
            if s == last:
                ring_copy(p, way, last, lax.rem(z + Z // 2, Z)).wait_recv()

    places = ((0, sib), (1, c), (1, sib), (-1, c), (-1, sib), (2, c), (2, sib))

    def spread_piece():
        for dy, cc in places:
            hh = yhead(dy, cc)
            remote(fg.at[h, pl.ds(pl.multiple_of(hh * PIECE, PIECE), PIECE), :], fgp.at[h],
                   y_send.at[hh], y_recv.at[h], at_h(hh)).start()
        fgp[h] = fg[h, my_piece, :]

    def pass_piece(zz):
        @pl.when(zz != z)
        def _():
            remote(fgp.at[zz], gz.at[z, my_piece, :], p_send.at[zz], p_recv.at[z], at_z(zz)).start()

        @pl.when(zz == z)
        def _():
            gz[z, my_piece, :] = fgp[zz]

    def pass_pieces():
        for dy, cc in places:
            hh = yhead(dy, cc)
            remote(fgp.at[hh], fgp.at[hh], y_send.at[hh], y_recv.at[hh], at_h(hh)).wait_recv()
            pass_piece(hh)

    for load in loads[:4]:
        load.wait()
    r_own = r_ref[x]
    row_power = [power(r_own, float(B * i)) for i in range(X)]
    z_power = [power(r_own, float(X * B * i)) for i in range(Z - 1)]
    for j in range(X):
        decayed = (head(k, j).astype(F32) * jnp.exp(-r_ref[j] * (B - 1.0 - rows))).astype(BF16)
        ts[0, j] = dot(decayed, head(v, j), 0, 0).astype(BF16)
    pl.semaphore_wait(barrier, len(peers))

    def partial(p, xx, part_at):
        at = lax.rem(xx + X, X) * CH + part_at * (CH // 2)
        return dot(gzt[pl.ds(pl.multiple_of(at, CH // 2), CH // 2), :], ab[p].reshape(Z * B, 2 * E))

    def share(p, way, i):
        return remote(dws.at[p, way, i], dwr.at[p, way, i], d_send.at[p, way, i], d_recv.at[p, way, i],
                      at_x(lax.rem(x + (X - 1 if way else 1), X)))

    def wait_pieces():
        for zz in range(Z):
            @pl.when(zz != z)
            def _():
                remote(gz.at[zz, my_piece, :], gz.at[zz, my_piece, :], p_send.at[zz], p_recv.at[zz], at_z(zz)).wait_recv()

    def from_sibling(n, *which):
        for i in which:
            gather_across(n, i)

    def head_grad_part(*distances):
        for dy in distances:
            for cc in range(2):
                hh = yhead(dy, cc)
                hacc[...] += dot(fg[hh], w[pl.ds(pl.multiple_of(hh * D8, D8), D8), :])

    def head_grad_start():
        loads[5].wait()
        hacc[...] = jnp.zeros_like(hacc)
        head_grad_part(0)

    def head_grad_end():
        head_grad_part(2)
        hg[...] = hacc[...].astype(BF16)

    def attention_scores():
        loads[4].wait()
        for j in range(X):
            sc[j] = (dot(head(q, j), head(k, j), 1, 1) * weights(j)).astype(BF16)

    def attention_start():
        for j in range(X):
            decay[j] = jnp.exp(-r_ref[j] * (rows + 1.0))
            intra[0, j] = dot(sc[j], head(v, j))

    def attention(p):
        for j in (2 * p, 2 * p + 1):
            inter = decay[j] * dot(head(q, j), st[0, j])
            ab[p, z, :, (j % 2) * E:(j % 2 + 1) * E] = (inter + intra[0, j]).astype(BF16)
        ring(0, p)

    def query_terms():
        for j in range(X):
            decayed = (head(q, j).astype(F32) * jnp.exp(-r_ref[j] * rows)).astype(BF16)
            ts[1, j] = dot(decayed, head(hg, j), 0, 0).astype(BF16)

    def query_grads():
        for j in range(X):
            gs[j] = (dot(head(hg, j), head(v, j), 1, 1) * weights(j)).astype(BF16)
            inter = decay[j] * dot(head(hg, j), st[0, j], 1, 1)
            qg_ref[:, j * E:(j + 1) * E] = (inter + dot(gs[j], head(k, j))).astype(BF16)

    def turn():
        for zz in range(Z):
            gzt[:, zz * B:(zz + 1) * B] = gz[zz].T

    def share_first(p):
        for way in range(2):
            dws[p, way, 0] = partial(p, x + 2, way).astype(BF16)
            share(p, way, 0).start()

    def share_direct(p):
        for way in range(2):
            dws[p, way, 1] = partial(p, x + (X - 1 if way else 1), 1 - way).astype(BF16)
            share(p, way, 1).start()

    def share_second(p):
        for way in range(2):
            own = partial(p, x + (X - 1 if way else 1), way)
            share(p, way, 0).wait_recv()
            dws[p, way, 2] = (own + dwr[p, way, 0].astype(F32)).astype(BF16)
            share(p, way, 2).start()

    def share_own():
        for p in range(2):
            for part_at in range(2):
                wg_ref[part_at * (CH // 2):(part_at + 1) * (CH // 2), p * 2 * E:(p + 1) * 2 * E] = partial(p, x, part_at)

    def key_value_start():
        for j in range(X):
            decay[j] = jnp.exp(-r_ref[j] * (B - rows))
            intra[0, j] = dot(gs[j], head(q, j), 0, 0)
            intra[1, j] = dot(sc[j], head(hg, j), 0, 0)

    def key_value_grads():
        for j in range(X):
            kg_ref[:, j * E:(j + 1) * E] = (
                decay[j] * dot(head(v, j), st[1, j], 1, 1) + intra[0, j]).astype(BF16)
            vg_ref[:, j * E:(j + 1) * E] = (
                decay[j] * dot(head(k, j), st[1, j]) + intra[1, j]).astype(BF16)

    def share_last(i, p):
        for way in range(2):
            part_at = 1 - way if i == 1 else way
            share(p, way, i).wait_recv()
            wg_ref[part_at * (CH // 2):(part_at + 1) * (CH // 2), p * 2 * E:(p + 1) * 2 * E] += dwr[p, way, i].astype(F32)

    def scan_sent(g):
        for o in range(1, X):
            remote(ts.at[g, 0], tx.at[g, 0], t_send.at[g, o - 1], t_recv.at[g, o - 1], at_x(x)).wait_send()
            remote(ss.at[g, 0], st.at[g, 0], s_send.at[g, o - 1], s_recv.at[g, o - 1], at_x(x)).wait_send()
        for d in range(1, Z):
            there = z - d if g else z + d
            ever = (there // half == z // half) | (z == half) if g else True

            @pl.when((there >= 0) & (there < Z) & ever)
            def _():
                remote(rs.at[g], rz.at[g, z], r_send.at[g, d - 1], r_recv.at[g, d - 1], at_z(there)).wait_send()

    def gather_sent(n):
        for i, part_at in enumerate((0, 1, 2, 3) * 3 + (None,) * 4):
            hop(n, h, part_at, i, up).wait_send()

    def pieces_sent():
        for zz in range(Z):
            @pl.when(zz != z)
            def _():
                remote(fgp.at[zz], gz.at[z, my_piece, :], p_send.at[zz], p_recv.at[z], at_z(zz)).wait_send()
        for dy, cc in places:
            hh = yhead(dy, cc)
            remote(fgp.at[hh], fgp.at[hh], y_send.at[hh], y_recv.at[hh], at_h(hh)).wait_send()

    def ring_sent():
        for p in range(2):
            for way in range(2):
                for s in range(last + 1):
                    ring_copy(p, way, s, z).wait_send()

    wide = [slice(p * 2 * E, (p + 1) * 2 * E) for p in range(2)]
    outs = [pltpu.make_async_copy(a, b, out_sem.at[i]) for i, (a, b) in enumerate(
        ((qg_ref, qg_hbm), (kg_ref, kg_hbm), (vg_ref, vg_hbm),
         (wg_ref.at[:, wide[0]], wg_hbm.at[:, wide[0]]), (wg_ref.at[:, wide[1]], wg_hbm.at[:, wide[1]])))]

    scan_send(0)
    spread_piece()
    gather_start(0)
    pass_piece(h)
    attention_scores()
    scan_rows(0)
    attention_start()
    gather_more(0)
    from_sibling(0, 0)
    head_grad_start()
    gather_forward(0)
    pass_pieces()
    gather_near(0)
    scan_finish(0)
    gather_far(0)
    from_sibling(0, 1, 2)
    head_grad_part(1, -1)
    scan_wait(0)
    attention(0)
    attention(1)
    wait_pieces()
    gather_start(1)
    from_sibling(0, 3)
    head_grad_end()
    query_terms()
    scan_send(1)
    gather_more(1)
    ring(1, 0)
    ring(1, 1)
    gather_forward(1)
    scan_rows(1)
    query_grads()
    outs[0].start()
    gather_near(1)
    ring(2, 0)
    ring(2, 1)
    scan_mid(1)
    gather_far(1)
    scan_sent(0)
    gather_sent(0)
    key_value_start()
    from_sibling(1, 0, 1, 2, 3)
    turn()
    ring(3, 0)
    share_first(0)
    ring(3, 1)
    share_first(1)
    share_direct(0)
    share_direct(1)
    scan_finish(1)
    share_second(0)
    share_second(1)
    share_own()
    pieces_sent()
    gather_sent(1)
    ring_sent()
    scan_wait(1)
    key_value_grads()
    share_last(1, 0)
    share_last(1, 1)
    outs[1].start()
    outs[2].start()
    share_last(2, 0)
    outs[3].start()
    share_last(2, 1)
    outs[4].start()

    scan_sent(1)
    for p in range(2):
        for way in range(2):
            for i in range(3):
                share(p, way, i).wait_send()
    for copy in outs:
        copy.wait()


def store(*refs):
    results, outs, held, in_sem, out_sem = refs[:4], refs[4:8], refs[8:12], refs[12], refs[13]
    loads = [pltpu.make_async_copy(a, b, in_sem.at[i]) for i, (a, b) in enumerate(zip(results, held))]
    stores = [pltpu.make_async_copy(a, b, out_sem.at[i]) for i, (a, b) in enumerate(zip(held, outs))]
    for load in loads:
        load.start()
    for load, copy in zip(loads, stores):
        load.wait()
        copy.start()
    for copy in stores:
        copy.wait()


def solution(mesh):
    Z, Y = mesh.shape["ctx"] // X, mesh.shape["head"] // 2
    H = 2 * Y

    def local(queries, key_vectors, value_vectors, out_grad, out_weight, decay_rate):
        B, C = queries.shape
        D8 = out_grad.shape[1]
        D = out_weight.shape[0]
        CH = D8 // X
        dma = pltpu.SemaphoreType.DMA
        vmem = pltpu.VMEM
        hbm = pl.BlockSpec(memory_space=pltpu.HBM)
        results = pl.pallas_call(
            functools.partial(kernel, Z, Y),
            out_shape=[jax.ShapeDtypeStruct((B, C), BF16)] * 3 + [jax.ShapeDtypeStruct((CH, C), F32)],
            in_specs=[hbm] * 6,
            out_specs=[hbm] * 4,
            scratch_shapes=[
                pltpu.SMEM((X,), F32),
                vmem((B, C), BF16), vmem((B, C), BF16), vmem((B, C), BF16), vmem((D, C), BF16),
                vmem((H, B, D8), BF16), vmem((Z, B, D8), BF16), vmem((D8, Z * B), BF16),
                vmem((B, C), BF16), vmem((B, C), F32),
                vmem((X, B, B), BF16), vmem((X, B, B), BF16),
                vmem((2, X, E, E), BF16), vmem((2, X, E, E), BF16),
                vmem((2, E, E), BF16), vmem((2, Z, E, E), BF16),
                vmem((2, X, E, E), BF16), vmem((2, X, E, E), BF16), vmem((E, E), F32),
                vmem((2, Z, B, 2 * E), BF16),
                vmem((2, 2, 3, CH // 2, 2 * E), BF16), vmem((2, 2, 3, CH // 2, 2 * E), BF16),
                vmem((H, B // H, D8), BF16),
                vmem((B, C), BF16), vmem((B, C), BF16), vmem((B, C), BF16), vmem((CH, C), F32),
                vmem((X, B, E), F32), vmem((2, X, B, E), F32),
                dma((6,)), dma((2, 16)), dma((2, 16)), dma((Z,)), dma((Z,)),
                dma((2, X - 1)), dma((2, X - 1)), dma((2, Z - 1)), dma((2, Z - 1)),
                dma((2, X - 1)), dma((2, X - 1)), dma((2, 2, Z // 2)), dma((2, 2, Z // 2)),
                dma((2, 2, 3)), dma((2, 2, 3)), dma((H,)), dma((H,)), dma((5,)),
            ],
            compiler_params=pltpu.CompilerParams(
                collective_id=0, has_side_effects=True, vmem_limit_bytes=63 * 1024 * 1024),
            name="lightning_backward",
        )(decay_rate, queries, key_vectors, value_vectors, out_grad, out_weight)
        return pl.pallas_call(
            store,
            out_shape=[jax.ShapeDtypeStruct(a.shape, a.dtype) for a in results],
            in_specs=[hbm] * 4,
            out_specs=[hbm] * 4,
            scratch_shapes=[vmem(a.shape, a.dtype) for a in results] + [dma((4,)), dma((4,))],
            compiler_params=pltpu.CompilerParams(vmem_limit_bytes=63 * 1024 * 1024),
            name="store_results",
        )(*results)

    tok = P("ctx", "head")
    return jax.shard_map(
        local, mesh=mesh, in_specs=(tok, tok, tok, tok, P(None, "head"), P("head")),
        out_specs=(tok, tok, tok, tok), check_vma=False)
```
